32 devices in a mesh: section: 4 (over y, core), dp: 2 (over x), tensor: 4 (over z).
Axes of the slice: x: 2, y: 2, z: 4, core: 2. Of those that a mesh axis runs over, the one named last changes fastest.
Arguments:
- cache: bfloat16 [4, 256, 5376], P('section'), may hold values from -6 to 6
- token_ids: int32 [128], replicated, may hold values from 0 to 255
- enc_weight: bfloat16 [4, 8192, 5376], P('section', ('dp', 'tensor')), may hold values from -0.078125 to 0.078125
- enc_bias: float32 [4, 8192], P('section', ('dp', 'tensor')), may hold values from -3 to 3
- dec_weight: bfloat16 [4, 4, 2688, 8192], P('section', None, ('dp', 'tensor')), may hold values from -0.09375 to 0.09375
- dec_bias: float32 [4, 2688], P('section', ('dp', 'tensor')), may hold values from -3 to 3
- incoming: float32 [4, 128, 2688], P('section', None, ('dp', 'tensor')), may hold values from -6 to 6
- target: bfloat16 [4, 128, 2688], P('section', None, ('dp', 'tensor')), may hold values from -6 to 6
- returned: bfloat16 [4, 128, 2688], P('section', None, ('dp', 'tensor')), may hold values from -6 to 6
Outputs:
- error: bfloat16 [4, 128, 2688], P('section', None, ('dp', 'tensor'))
- outgoing: float32 [4, 128, 2688], P('section', None, ('dp', 'tensor'))
- lat_grad: float32 [4, 8192, 128], P('section', ('dp', 'tensor'))
The draws below stay inside these ranges and needn't reach their ends.
All inputs are finite; a program needn't handle non-finite values.
Results may differ from the reference program's by a relative error of at most 0.014.
Values may be sent and summed in bfloat16 or wider, within the bound.
No kernel may reach another device: no remote copies, remote signals or barrier semaphores. Data moves between devices by JAX's collectives and lax.ppermute only.
A program may use at most 128 MiB of HBM per device.

```python
import jax
import jax.numpy as jnp

D = 5376
LAT = 8192
DO = 2688
TOKENS = 128
LAYERS = 4
CACHE_ROWS = 256


def touch_ends(array, stream_key, least, top_value):
    longest = array.shape.index(max(array.shape))
    spots = []
    for shift in (0, 1):
        where = [jax.random.randint(jax.random.fold_in(stream_key, axis), (), 0, length) for axis, length in enumerate(array.shape)]
        where[longest] = (where[longest] + shift) % array.shape[longest]
        spots.append(tuple(where))
    return array.at[spots[0]].set(least).at[spots[1]].set(top_value)


def spiked(values, own_key, source, target, blocks, factor):
    owner, partner = [(jnp.arange(values.shape[axis_at]) // (values.shape[axis_at] // blocks)).reshape([-1 if axis == axis_at else 1 for axis in range(values.ndim)]) for axis_at in (source, target)]
    chosen = jax.random.permutation(own_key, blocks)[partner]
    strong = (owner == chosen) | (owner == (partner + blocks // 2) % blocks)
    return jnp.where(strong, factor * values, values)


def block_scale(own_key, extent, cuts, least, largest):
    def one(dim, parts):
        steps = jax.random.uniform(jax.random.fold_in(jax.random.fold_in(own_key, 6), dim), (parts,), jnp.float32, least / len(cuts), largest / len(cuts))
        return jnp.repeat(jnp.exp(steps), extent[dim] // parts).reshape((-1,) + (1,) * (len(extent) - dim - 1))

    level = one(*cuts[0])
    for cut in cuts[1:]:
        level = level * one(*cut)
    return level


def scatter_about(stream_key, dims, width, most, cuts=(), dtype=jnp.bfloat16):
    drawn = jax.random.normal(stream_key, dims, jnp.float32) * width
    if len(cuts) > 0:
        drawn = block_scale(stream_key, dims, cuts, -0.22, 0.18) * drawn
    return jnp.clip(drawn, min=-most, max=most).astype(dtype)


def gaussian_with(key, shape, spread, limit, shards, heavy, dtype=jnp.bfloat16):
    values = spread * jax.random.normal(key, shape, jnp.float32)
    if shards:
        values = values * block_scale(key, shape, shards, -0.22, 0.18)
    return jnp.clip(spiked(values, jax.random.fold_in(key, 3), *heavy), -limit, limit).astype(dtype)


def setup_inputs(seed: int = 0) -> dict:
    key_of = jax.random.split(jax.random.key(seed), 10)
    return {
        "cache": scatter_about(key_of[0], (LAYERS, CACHE_ROWS, D), 1.0, 6.0, ((0, 4),)),
        "token_ids": touch_ends(jax.random.randint(key_of[1], (TOKENS,), 0, CACHE_ROWS), jax.random.fold_in(key_of[1], 1), 0, CACHE_ROWS - 1).astype(jnp.int32),
        "enc_weight": scatter_about(key_of[2], (LAYERS, LAT, D), D ** -0.5, 0.078125, ((0, 4), (1, 8))),
        "enc_bias": scatter_about(key_of[3], (LAYERS, LAT), 0.5, 3.0, ((0, 4), (1, 8)), jnp.float32),
        "dec_weight": gaussian_with(key_of[4], (LAYERS, LAYERS, DO, LAT), LAT ** -0.5, 0.09375, ((0, 4), (2, 8)), (3, 2, 8, 2.0)),
        "dec_bias": scatter_about(key_of[5], (LAYERS, DO), 0.5, 3.0, ((0, 4), (1, 8)), jnp.float32),
        "incoming": scatter_about(key_of[6], (LAYERS, TOKENS, DO), 1.0, 6.0, ((0, 4), (2, 8)), jnp.float32),
        "target": scatter_about(key_of[7], (LAYERS, TOKENS, DO), 1.0, 6.0, ((0, 4), (2, 8))),
        "returned": scatter_about(key_of[8], (LAYERS, TOKENS, DO), 1.0, 6.0, ((0, 4), (2, 8))),
    }


def reference(cache, token_ids, enc_weight, enc_bias, dec_weight, dec_bias, incoming, target, returned):
    layers = cache.shape[0]
    latent_list = []
    for layer in range(layers):
        rows = cache[layer][token_ids]
        pre = jnp.dot(rows, enc_weight[layer].T, preferred_element_type=jnp.float32) + enc_bias[layer]
        latent_list.append(jnp.maximum(pre, 0.0).astype(jnp.bfloat16))
    recon = [incoming[layer] + dec_bias[layer] for layer in range(layers)]
    outgo = [jnp.zeros(incoming.shape[1:], jnp.float32) for layer in range(layers)]
    for layer in range(layers):
        for offset in range(layers):
            part = jnp.dot(latent_list[layer], dec_weight[layer, offset].T, preferred_element_type=jnp.float32)
            where_to = layer + offset
            if where_to < layers:
                recon[where_to] = recon[where_to] + part
            else:
                outgo[where_to - layers] = outgo[where_to - layers] + part
    error = jnp.stack([recon[t] - target[t].astype(jnp.float32) for t in range(layers)]).astype(jnp.bfloat16)
    outgoing = jnp.stack(outgo)
    grads = []
    for layer in range(layers):
        total = jnp.zeros((dec_weight.shape[3], incoming.shape[1]), jnp.float32)
        for offset in range(layers):
            where_to = layer + offset
            if where_to < layers:
                upstream = error[where_to]
            else:
                upstream = returned[where_to - layers]
            total = total + jnp.dot(dec_weight[layer, offset].T, upstream.T, preferred_element_type=jnp.float32)
        grads.append(total)
    return error, outgoing, jnp.stack(grads)
```

```python
import jax
import jax.numpy as jnp
from jax import lax
from jax.sharding import PartitionSpec as P

GROUP = ("dp", "tensor")
BF16 = jnp.bfloat16
F32 = jnp.float32


def cycle_order(rows, columns):
    order = []
    for row in range(rows):
        line = [row * columns + column for column in range(columns)]
        order += line if row % 2 == 0 else line[::-1]
    return order


def local(cache, token_ids, enc_weight, enc_bias, dec_weight, dec_bias, incoming, target, returned):
    layers = lax.axis_size("section")
    section = lax.axis_index("section")
    order = cycle_order(lax.axis_size("dp"), lax.axis_size("tensor"))
    size = len(order)
    place_of = [order.index(i) for i in range(size)]
    me = lax.axis_index(GROUP)
    place = jnp.asarray(place_of, jnp.int32)[me]

    def along(value, by):
        pairs = [(order[i], order[(i + by) % size]) for i in range(size)]
        return lax.ppermute(value, GROUP, pairs)

    def member(distance):
        return jnp.asarray(order, jnp.int32)[(place + distance) % size]

    def shifted(value, by):
        return lax.ppermute(value, "section", [(i, (i + by) % layers) for i in range(layers)])

    mine = enc_weight.shape[1]
    half = mine // 2
    columns = dec_weight.shape[2]
    tokens = token_ids.shape[0]
    decoders = dec_weight[0].reshape(layers * columns, dec_weight.shape[3])

    def part(owner, which):
        return lax.dynamic_slice_in_dim(decoders, owner * mine + which * half, half, 1)

    rows = cache[0].at[token_ids].get(mode="promise_in_bounds")

    def encode(which):
        pre = lax.dot_general(
            rows,
            enc_weight[0, which * half : (which + 1) * half],
            (((1,), (1,)), ((), ())),
            preferred_element_type=F32,
        )
        bias = enc_bias[0, which * half : (which + 1) * half]
        return jnp.maximum(pre + bias, 0.0).astype(BF16)

    def decode(latents, owner, which):
        return lax.dot_general(
            part(owner, which), latents, (((1,), (1,)), ((), ())), preferred_element_type=F32
        )

    own = [encode(0), encode(1)]
    total = decode(own[0], me, 0) + decode(own[1], me, 1)
    up, down = list(own), list(own)
    for step in range(1, (size - 1) // 2 + 1):
        for which in (0, 1):
            up[which] = along(up[which], 1)
            down[which] = along(down[which], -1)
            total = total + decode(up[which], member(-step), which)
            total = total + decode(down[which], member(step), which)
    if size % 2 == 0:
        total = total + decode(along(up[0], 1), member(size // 2), 0)
        total = total + decode(along(down[1], -1), member(size // 2), 1)

    by_offset = total.reshape(layers, columns, tokens)
    within = by_offset[0]
    beyond = jnp.zeros_like(within)
    for offset in range(1, layers):
        came = shifted(by_offset[offset].astype(BF16), offset).astype(F32)
        within = within + jnp.where(section >= offset, came, 0.0)
        beyond = beyond + jnp.where(section < offset, came, 0.0)
    recon = within + incoming[0].T + dec_bias[0][:, None]
    error = (recon - target[0].T.astype(F32)).astype(BF16)
    passed = returned[0].T
    upstream = [error]
    for offset in range(1, layers):
        upstream.append(shifted(jnp.where(section >= offset, error, passed), -offset))
    back = jnp.concatenate(upstream, 0)

    def gradient(owner, which):
        return lax.dot_general(
            part(owner, which), back, (((0,), (0,)), ((), ())), preferred_element_type=F32
        )

    up, down = [None, None], [None, None]
    if size % 2 == 0:
        up[0] = along(gradient(member(size // 2), 0).astype(BF16), 1)
        down[1] = along(gradient(member(size // 2), 1).astype(BF16), -1)
    for step in range((size - 1) // 2, 0, -1):
        for which in (0, 1):
            rise = gradient(member(step), which)
            fall = gradient(member(-step), which)
            if up[which] is not None:
                rise = rise + up[which].astype(F32)
            if down[which] is not None:
                fall = fall + down[which].astype(F32)
            up[which] = along(rise.astype(BF16), 1)
            down[which] = along(fall.astype(BF16), -1)
    parts = []
    for which in (0, 1):
        own_part = gradient(me, which)
        for came in (up[which], down[which]):
            if came is not None:
                own_part = own_part + came.astype(F32)
        parts.append(own_part)
    lat_grad = jnp.concatenate(parts, 0)
    return (error.T[None], beyond.T[None], lat_grad[None])


def solution(mesh):
    placed = (
        P("section", None, None),
        P(),
        P("section", GROUP, None),
        P("section", GROUP),
        P("section", None, GROUP, None),
        P("section", GROUP),
        P("section", None, GROUP),
        P("section", None, GROUP),
        P("section", None, GROUP),
    )
    return jax.shard_map(
        local,
        mesh=mesh,
        in_specs=placed,
        out_specs=(
            P("section", None, GROUP),
            P("section", None, GROUP),
            P("section", GROUP, None),
        ),
        check_vma=False,
    )
```

```python
import functools

import jax
import jax.numpy as jnp
from jax import lax
from jax.experimental import pallas as pl
from jax.experimental.pallas import tpu as pltpu
from jax.sharding import PartitionSpec as P

GROUP = ("dp", "tensor")
BF16 = jnp.bfloat16
F32 = jnp.float32
VMEM = pl.BlockSpec(memory_space=pltpu.VMEM)
SMEM = pl.BlockSpec(memory_space=pltpu.SMEM)
HBM = pl.BlockSpec(memory_space=pltpu.HBM)
NT = (((1,), (1,)), ((), ()))
TN = (((0,), (0,)), ((), ()))


def cycle_order(rows, columns):
    order = []
    for row in range(rows):
        line = [row * columns + column for column in range(columns)]
        order += line if row % 2 == 0 else line[::-1]
    return order


def ring_tools():
    order = cycle_order(lax.axis_size("dp"), lax.axis_size("tensor"))
    size = len(order)
    layers = lax.axis_size("section")

    def along(value, by):
        pairs = [(order[i], order[(i + by) % size]) for i in range(size)]
        return lax.ppermute(value, GROUP, pairs)

    def shifted(value, by):
        return lax.ppermute(value, "section", [(i, (i + by) % layers) for i in range(layers)])

    return order, along, shifted


def call(kernel, name, outs, operands, specs, scratch=(), limit=4, flops=0, bytes_accessed=0):
    return pl.pallas_call(
        kernel,
        out_shape=[pltpu.VMEM(shape, dtype) for shape, dtype in outs],
        in_specs=specs,
        out_specs=[VMEM] * len(outs),
        scratch_shapes=list(scratch),
        compiler_params=pltpu.CompilerParams(vmem_limit_bytes=limit * 2**20),
        cost_estimate=pl.CostEstimate(
            flops=flops, bytes_accessed=bytes_accessed, transcendentals=0
        ),
        name=name,
    )(*operands)


def gather_encode_kernel(ids, cache, weight, bias, rows, latents, held, blocks, sems, *, first, block):
    count = latents.shape[1] // block
    copies = [pltpu.make_async_copy(cache.at[0], held, sems.at[0])]
    for i in range(count):
        source = weight.at[0, pl.ds(first + i * block, block)]
        copies.append(pltpu.make_async_copy(source, blocks.at[i], sems.at[i + 1]))
    for copy in copies:
        copy.start()
    slots = lax.broadcasted_iota(jnp.int32, (held.shape[0], ids.shape[1]), 0)
    picked = (slots == ids[...]).astype(F32).astype(BF16)
    copies[0].wait()
    rows[...] = lax.dot_general(picked, held[...], TN, preferred_element_type=F32).astype(BF16)
    for i in range(count):
        copies[i + 1].wait()
        pre = lax.dot_general(rows[...], blocks[i], NT, preferred_element_type=F32)
        pre = pre + bias[:, first + i * block : first + (i + 1) * block]
        latents[:, i * block : (i + 1) * block] = jnp.maximum(pre, 0.0).astype(BF16)


def encode_kernel(rows, weight, bias, latents, blocks, sems, *, first, block):
    count = latents.shape[1] // block
    copies = []
    for i in range(count):
        source = weight.at[0, pl.ds(first + i * block, block)]
        copies.append(pltpu.make_async_copy(source, blocks.at[i], sems.at[i]))
    for copy in copies:
        copy.start()
    for i in range(count):
        copies[i].wait()
        pre = lax.dot_general(rows[...], blocks[i], NT, preferred_element_type=F32)
        pre = pre + bias[:, first + i * block : first + (i + 1) * block]
        latents[:, i * block : (i + 1) * block] = jnp.maximum(pre, 0.0).astype(BF16)


def columns_of(decoders, owner, which, half):
    start = pl.multiple_of(owner * (2 * half) + which * half, half)
    return decoders[:, pl.ds(start, half)]


def decoded(meta, decoders, pieces, half):
    total = None
    for distance, which, piece in pieces:
        columns = columns_of(decoders, meta[distance], which, half)
        part = lax.dot_general(columns, piece[...], NT, preferred_element_type=F32)
        total = part if total is None else total + part
    return total


def decode_first_kernel(meta, decoders, low, high, incoming, bias, target, total, base):
    half = low.shape[1]
    total[...] = decoded(meta, decoders, [(0, 0, low), (0, 1, high)], half)
    base[...] = incoming[...] + bias[...] - target[...].astype(F32)


def decode_kernel(meta, decoders, before, one, other, total, *, pieces):
    half = one.shape[1]
    (d0, w0), (d1, w1) = pieces
    total[...] = before[...] + decoded(meta, decoders, [(d0, w0, one), (d1, w1, other)], half)


def decode_last_kernel(meta, decoders, before, one, other, own, *sent, pieces):
    half = one.shape[1]
    (d0, w0), (d1, w1) = pieces
    total = before[...] + decoded(meta, decoders, [(d0, w0, one), (d1, w1, other)], half)
    rows = own.shape[0]
    own[...] = total[:rows]
    for offset, out in enumerate(sent, 1):
        out[...] = total[offset * rows : (offset + 1) * rows].astype(BF16)


def error_kernel(meta, own, base, returned, *refs, layers, slot):
    came, (error, beyond, *sent) = refs[: layers - 1], refs[layers - 1 :]
    section = meta[slot]
    within = own[...] + base[...]
    after = jnp.zeros_like(within)
    for offset in range(1, layers):
        part = came[offset - 1][...].astype(F32)
        inside = section >= offset
        within = within + jnp.where(inside, part, 0.0)
        after = after + jnp.where(inside, 0.0, part)
    mine = within.astype(BF16)
    error[...] = mine
    beyond[...] = after
    passed = returned[...]
    for offset in range(1, layers):
        sent[offset - 1][...] = jnp.where(section >= offset, mine, passed)


def gradient(meta, decoders, back, distance, which, half):
    columns = columns_of(decoders, meta[distance], which, half)
    return lax.dot_general(back[...], columns, TN, preferred_element_type=F32)


def gradient_first_kernel(meta, decoders, *refs, layers, pieces, half):
    parts, (back, *outs) = refs[:layers], refs[layers:]
    rows = parts[0].shape[0]
    for offset in range(layers):
        back[offset * rows : (offset + 1) * rows] = parts[offset][...]
    for (distance, which), out in zip(pieces, outs):
        out[...] = gradient(meta, decoders, back, distance, which, half).astype(BF16)


def gradient_kernel(meta, decoders, back, *refs, pieces, half):
    count = len(pieces)
    came, outs = refs[:-count], refs[-count:]
    for i, (distance, which) in enumerate(pieces):
        total = gradient(meta, decoders, back, distance, which, half)
        if came:
            total = total + came[i][...].astype(F32)
        outs[i][...] = total.astype(BF16)


def gradient_own_kernel(meta, decoders, back, low, high, total, *, half):
    for which, came in ((0, low), (1, high)):
        part = gradient(meta, decoders, back, 0, which, half) + came[...].astype(F32)
        total[:, which * half : (which + 1) * half] = part


def gradient_last_kernel(before, low, high, out):
    half = low.shape[1]
    for which, came in ((0, low), (1, high)):
        part = before[:, which * half : (which + 1) * half] + came[...].astype(F32)
        out[which * half : (which + 1) * half, :] = part.T


def tiled_local(cache, token_ids, enc_weight, enc_bias, dec_weight, dec_bias, incoming, target, returned):
    order, along, shifted = ring_tools()
    size = len(order)
    far = size // 2
    layers = lax.axis_size("section")
    rows_, line = lax.axis_size("dp"), lax.axis_size("tensor")
    tokens = token_ids.shape[0]
    slots, width = cache.shape[1:]
    mine = enc_weight.shape[1]
    half = mine // 2
    columns = dec_weight.shape[2]
    outs_all = layers * columns

    def snake(index):
        row, column = index // line, index % line
        return row * line + jnp.where(row % 2 == 0, column, line - 1 - column)

    place = snake(lax.axis_index(GROUP))
    members = snake((place + jnp.arange(size, dtype=jnp.int32)) % size)
    meta = jnp.concatenate([members, lax.axis_index("section").reshape(1)]).astype(jnp.int32)

    weight = pltpu.with_memory_space_constraint(enc_weight, pltpu.HBM)
    kept = pltpu.with_memory_space_constraint(cache, pltpu.HBM)
    decoders = dec_weight.reshape(outs_all, dec_weight.shape[3])

    block = min(256, half)
    count = half // block
    rows, low = call(
        functools.partial(gather_encode_kernel, first=0, block=block),
        "encode_low",
        [((tokens, width), BF16), ((tokens, half), BF16)],
        (token_ids.reshape(1, tokens), kept, weight, enc_bias),
        [VMEM, HBM, HBM, VMEM],
        [
            pltpu.VMEM((slots, width), BF16),
            pltpu.VMEM((count, block, width), BF16),
            pltpu.SemaphoreType.DMA((count + 1,)),
        ],
        limit=16,
        flops=2 * tokens * width * (half + slots),
        bytes_accessed=2 * width * (half + slots),
    )
    (high,) = call(
        functools.partial(encode_kernel, first=half, block=block),
        "encode_high",
        [((tokens, half), BF16)],
        (rows, weight, enc_bias),
        [VMEM, HBM, VMEM],
        [pltpu.VMEM((count, block, width), BF16), pltpu.SemaphoreType.DMA((count,))],
        limit=16,
        flops=2 * tokens * width * half,
        bytes_accessed=2 * width * half,
    )
    piece_flops = 2 * tokens * half * outs_all
    own_low, own_high = low, high
    total, base = call(
        decode_first_kernel,
        "decode_own",
        [((outs_all, tokens), F32), ((columns, tokens), F32)],
        (
            meta,
            decoders,
            own_low,
            own_high,
            incoming[0].T,
            dec_bias.reshape(columns, 1),
            target[0].T,
        ),
        [SMEM] + [VMEM] * 6,
        flops=2 * piece_flops,
    )
    up, down = [low, high], [low, high]
    for step in range(1, far):
        for which in (0, 1):
            up[which] = along(up[which], 1)
            down[which] = along(down[which], -1)
            (total,) = call(
                functools.partial(
                    decode_kernel, pieces=((size - step, which), (step, which))
                ),
                f"decode_{step}_{which}",
                [((outs_all, tokens), F32)],
                (meta, decoders, total, up[which], down[which]),
                [SMEM] + [VMEM] * 4,
                flops=2 * piece_flops,
            )
    own, *sent = call(
        functools.partial(decode_last_kernel, pieces=((far, 0), (far, 1))),
        "decode_last",
        [((columns, tokens), F32)] + [((columns, tokens), BF16)] * (layers - 1),
        (meta, decoders, total, along(up[0], 1), along(down[1], -1)),
        [SMEM] + [VMEM] * 4,
        flops=2 * piece_flops,
    )
    came = [shifted(value, offset) for offset, value in enumerate(sent, 1)]
    error, beyond, *sent = call(
        functools.partial(error_kernel, layers=layers, slot=size),
        "error",
        [((columns, tokens), BF16), ((columns, tokens), F32)]
        + [((columns, tokens), BF16)] * (layers - 1),
        (meta, own, base, returned[0].T, *came),
        [SMEM] + [VMEM] * (layers + 2),
    )
    came = [shifted(value, -offset) for offset, value in enumerate(sent, 1)]
    piece = ((tokens, half), BF16)
    back, *first = call(
        functools.partial(
            gradient_first_kernel, layers=layers, pieces=((far, 0), (far, 1)), half=half
        ),
        "gradient_far",
        [((outs_all, tokens), BF16), piece, piece],
        (meta, decoders, error, *came),
        [SMEM] + [VMEM] * (layers + 1),
        flops=2 * piece_flops,
    )
    outer, inner = first, []
    for step in range(far - 1, -1, -1):
        if outer:
            outer = [along(outer[0], 1), along(outer[1], -1)]
        if step == 0:
            break
        inner = call(
            functools.partial(
                gradient_kernel, pieces=((size - step, 0), (step, 1)), half=half
            ),
            f"gradient_inner_{step}",
            [piece, piece],
            (meta, decoders, back, *inner),
            [SMEM] + [VMEM] * (2 + len(inner)),
            flops=2 * piece_flops,
        )
        inner = [along(inner[0], -1), along(inner[1], 1)]
        outer = call(
            functools.partial(
                gradient_kernel, pieces=((step, 0), (size - step, 1)), half=half
            ),
            f"gradient_outer_{step}",
            [piece, piece],
            (meta, decoders, back, *outer),
            [SMEM] + [VMEM] * (2 + len(outer)),
            flops=2 * piece_flops,
        )
    (part,) = call(
        functools.partial(gradient_own_kernel, half=half),
        "gradient_own",
        [((tokens, mine), F32)],
        (meta, decoders, back, *inner),
        [SMEM] + [VMEM] * 4,
        flops=2 * piece_flops,
    )
    lat_grad = pl.pallas_call(
        gradient_last_kernel,
        out_shape=jax.ShapeDtypeStruct((mine, tokens), F32),
        in_specs=[VMEM] * 3,
        out_specs=VMEM,
        compiler_params=pltpu.CompilerParams(vmem_limit_bytes=4 * 2**20),
        name="gradient_last",
    )(part, *outer)
    return (error.T[None], beyond.T[None], lat_grad[None])


def plain_local(cache, token_ids, enc_weight, enc_bias, dec_weight, dec_bias, incoming, target, returned):
    order, along, shifted = ring_tools()
    size = len(order)
    layers = lax.axis_size("section")
    section = lax.axis_index("section")
    place = jnp.asarray([order.index(i) for i in range(size)], jnp.int32)[lax.axis_index(GROUP)]
    mine = enc_weight.shape[1]
    columns = dec_weight.shape[2]
    tokens = token_ids.shape[0]
    halves = [slice(0, mine // 2), slice(mine // 2, mine)]
    decoders = dec_weight[0].reshape(layers * columns, dec_weight.shape[3])

    def member(distance):
        return jnp.asarray(order, jnp.int32)[(place + distance) % size]

    def part(owner, which):
        start, length = halves[which].start, halves[which].stop - halves[which].start
        return lax.dynamic_slice_in_dim(decoders, owner * mine + start, length, 1)

    def decode(latents, owner, which):
        return lax.dot_general(part(owner, which), latents, NT, preferred_element_type=F32)

    rows = cache[0].at[token_ids].get(mode="promise_in_bounds")
    pre = lax.dot_general(rows, enc_weight[0], NT, preferred_element_type=F32)
    latents = jnp.maximum(pre + enc_bias[0], 0.0).astype(BF16)
    up = [latents[:, cut] for cut in halves]
    down = list(up)
    total = decode(up[0], member(0), 0) + decode(up[1], member(0), 1)
    for step in range(1, (size - 1) // 2 + 1):
        for which in (0, 1):
            up[which] = along(up[which], 1)
            down[which] = along(down[which], -1)
            total = total + decode(up[which], member(-step), which)
            total = total + decode(down[which], member(step), which)
    if size % 2 == 0:
        total = total + decode(along(up[0], 1), member(size // 2), 0)
        total = total + decode(along(down[1], -1), member(size // 2), 1)

    by_offset = total.reshape(layers, columns, tokens)
    within = by_offset[0]
    beyond = jnp.zeros_like(within)
    for offset in range(1, layers):
        came = shifted(by_offset[offset].astype(BF16), offset).astype(F32)
        within = within + jnp.where(section >= offset, came, 0.0)
        beyond = beyond + jnp.where(section < offset, came, 0.0)
    recon = within + incoming[0].T + dec_bias[0][:, None]
    error = (recon - target[0].T.astype(F32)).astype(BF16)
    passed = returned[0].T
    upstream = [error]
    for offset in range(1, layers):
        upstream.append(shifted(jnp.where(section >= offset, error, passed), -offset))
    back = jnp.concatenate(upstream, 0)

    def gradient_of(owner, which):
        return lax.dot_general(part(owner, which), back, TN, preferred_element_type=F32)

    up, down = [None, None], [None, None]
    if size % 2 == 0:
        up[0] = along(gradient_of(member(size // 2), 0).astype(BF16), 1)
        down[1] = along(gradient_of(member(size // 2), 1).astype(BF16), -1)
    for step in range((size - 1) // 2, 0, -1):
        for which in (0, 1):
            rise = gradient_of(member(step), which)
            fall = gradient_of(member(-step), which)
            if up[which] is not None:
                rise = rise + up[which].astype(F32)
            if down[which] is not None:
                fall = fall + down[which].astype(F32)
            up[which] = along(rise.astype(BF16), 1)
            down[which] = along(fall.astype(BF16), -1)
    parts = []
    for which in (0, 1):
        own_part = gradient_of(member(0), which)
        for came in (up[which], down[which]):
            if came is not None:
                own_part = own_part + came.astype(F32)
        parts.append(own_part)
    lat_grad = jnp.concatenate(parts, 0)
    return (error.T[None], beyond.T[None], lat_grad[None])


def local(cache, token_ids, enc_weight, enc_bias, dec_weight, *rest):
    size = lax.axis_size("dp") * lax.axis_size("tensor")
    mine, width = enc_weight.shape[1:]
    whole_tiles = (
        size % 2 == 0
        and size >= 4
        and mine % 256 == 0
        and width % 128 == 0
        and dec_weight.shape[2] % 16 == 0
        and token_ids.shape[0] % 128 == 0
        and cache.shape[1] % 16 == 0
    )
    form = tiled_local if whole_tiles else plain_local
    return form(cache, token_ids, enc_weight, enc_bias, dec_weight, *rest)


def solution(mesh):
    placed = (
        P("section", None, None),
        P(),
        P("section", GROUP, None),
        P("section", GROUP),
        P("section", None, GROUP, None),
        P("section", GROUP),
        P("section", None, GROUP),
        P("section", None, GROUP),
        P("section", None, GROUP),
    )
    return jax.shard_map(
        local,
        mesh=mesh,
        in_specs=placed,
        out_specs=(
            P("section", None, GROUP),
            P("section", None, GROUP),
            P("section", GROUP, None),
        ),
        check_vma=False,
    )
```

```python
import functools

import jax
import jax.numpy as jnp
from jax import lax
from jax.experimental import pallas as pl
from jax.experimental.pallas import tpu as pltpu
from jax.sharding import PartitionSpec as P

GROUP = ("dp", "tensor")
BF16 = jnp.bfloat16
F32 = jnp.float32
VMEM = pl.BlockSpec(memory_space=pltpu.VMEM)
HBM = pl.BlockSpec(memory_space=pltpu.HBM)
NT = (((1,), (1,)), ((), ()))
TN = (((0,), (0,)), ((), ()))


def cycle_order(rows, columns):
    order = []
    for row in range(rows):
        line = [row * columns + column for column in range(columns)]
        order += line if row % 2 == 0 else line[::-1]
    return order


def ring_tools():
    order = cycle_order(lax.axis_size("dp"), lax.axis_size("tensor"))
    size = len(order)
    layers = lax.axis_size("section")

    def along(value, by):
        pairs = [(order[i], order[(i + by) % size]) for i in range(size)]
        return lax.ppermute(value, GROUP, pairs)

    def shifted(value, by):
        return lax.ppermute(value, "section", [(i, (i + by) % layers) for i in range(layers)])

    return order, along, shifted


def call(kernel, name, outs, operands, specs, scratch=(), limit=4, flops=0, bytes_accessed=0):
    return pl.pallas_call(
        kernel,
        out_shape=[pltpu.VMEM(shape, dtype) for shape, dtype in outs],
        in_specs=specs,
        out_specs=[VMEM] * len(outs),
        scratch_shapes=list(scratch),
        compiler_params=pltpu.CompilerParams(vmem_limit_bytes=limit * 2**20),
        cost_estimate=pl.CostEstimate(
            flops=flops, bytes_accessed=bytes_accessed, transcendentals=0
        ),
        name=name,
    )(*operands)


def owner_at(distance):
    rows, line = lax.axis_size("dp"), lax.axis_size("tensor")

    def snake(index):
        row, column = index // line, index % line
        return row * line + jnp.where(row % 2 == 0, column, line - 1 - column)

    place = snake(lax.axis_index("dp") * line + lax.axis_index("tensor"))
    return snake((place + distance) % (rows * line))


def columns_of(decoders, distance, which, half):
    start = owner_at(distance) * (2 * half) + which * half
    return decoders[:, pl.ds(pl.multiple_of(start, half), half)]


def upright(row, lanes):
    return jnp.broadcast_to(row, (lanes, row.shape[1])).T


def encode_kernel(ids, cache, weight, bias, low, high, ids_, held, blocks, bias_, across, sems):
    count, block = blocks.shape[:2]
    tokens, half = across.shape[1], low.shape[0]
    copies = [
        pltpu.make_async_copy(ids, ids_.at[0], sems.at[count]),
        pltpu.make_async_copy(cache.at[0], held, sems.at[count + 1]),
        pltpu.make_async_copy(bias, bias_, sems.at[count + 2]),
    ]
    for copy in copies:
        copy.start()
    streams = []
    for i in range(count):
        source = weight.at[0, pl.ds(i * block, block)]
        streams.append(pltpu.make_async_copy(source, blocks.at[i], sems.at[i]))
        streams[i].start()
    copies[0].wait()
    slots = lax.broadcasted_iota(jnp.int32, (held.shape[0], tokens), 0)
    picked = (slots == ids_[...]).astype(F32).astype(BF16)
    copies[1].wait()
    rows = lax.dot_general(picked, held[...], TN, preferred_element_type=F32)
    across[...] = rows.astype(BF16).T
    copies[2].wait()
    for i in range(count):
        streams[i].wait()
        pre = jnp.dot(blocks[i], across[...], preferred_element_type=F32)
        pre = pre + upright(bias_[:, i * block : (i + 1) * block], tokens)
        out = low if (i + 1) * block <= half else high
        start = i * block % half
        out[start : start + block] = jnp.maximum(pre, 0.0).astype(BF16)


def decoded(decoders, pieces):
    total = None
    for distance, which, piece in pieces:
        columns = columns_of(decoders, distance, which, piece.shape[0])
        part = jnp.dot(columns, piece[...], preferred_element_type=F32)
        total = part if total is None else total + part
    return total


def load_decode_kernel(source, low, high, decoders, total, sems):
    layers = sems.shape[0]
    rows = source.shape[0] // layers
    copies = []
    for i in range(layers):
        part = pl.ds(i * rows, rows)
        copies.append(pltpu.make_async_copy(source.at[part], decoders.at[part], sems.at[i]))
        copies[i].start()
    for i in range(layers):
        part = pl.ds(i * rows, rows)
        copies[i].wait()
        total[part] = decoded(decoders.at[part], [(0, 0, low), (0, 1, high)])


def decode_kernel(decoders, before, one, other, total, *, pieces):
    (d0, w0), (d1, w1) = pieces
    total[...] = before[...] + decoded(decoders, [(d0, w0, one), (d1, w1, other)])


def decode_last_kernel(decoders, before, one, other, own, *sent, pieces):
    (d0, w0), (d1, w1) = pieces
    total = before[...] + decoded(decoders, [(d0, w0, one), (d1, w1, other)])
    rows = own.shape[0]
    own[...] = total[:rows]
    for offset, out in enumerate(sent, 1):
        out[...] = total[offset * rows : (offset + 1) * rows].astype(BF16)


def error_kernel(own, incoming, bias, target, returned, *refs, layers):
    came, (error, beyond, *sent) = refs[: layers - 1], refs[layers - 1 :]
    section = lax.axis_index("section")
    shift = upright(bias[...], incoming.shape[1])
    within = own[...] + (incoming[...] + shift) - target[...].astype(F32)
    after = jnp.zeros_like(within)
    for offset in range(1, layers):
        part = came[offset - 1][...].astype(F32)
        inside = section >= offset
        within = within + jnp.where(inside, part, 0.0)
        after = after + jnp.where(inside, 0.0, part)
    mine = within.astype(BF16)
    error[...] = mine
    beyond[...] = after
    passed = returned[...]
    for offset in range(1, layers):
        sent[offset - 1][...] = jnp.where(section >= offset, mine, passed)


def gradient(decoders, back, distance, which, half):
    columns = columns_of(decoders, distance, which, half)
    return jnp.dot(back[...], columns, preferred_element_type=F32)


def gradient_first_kernel(decoders, *refs, layers, pieces):
    parts, (back, *outs) = refs[:layers], refs[layers:]
    back[...] = jnp.concatenate([part[...] for part in parts], 0).T
    for (distance, which), out in zip(pieces, outs):
        out[...] = gradient(decoders, back, distance, which, out.shape[1]).astype(BF16)


def gradient_kernel(decoders, back, *refs, pieces):
    count = len(pieces)
    came, outs = refs[:-count], refs[-count:]
    for i, (distance, which) in enumerate(pieces):
        total = gradient(decoders, back, distance, which, outs[i].shape[1])
        if came:
            total = total + came[i][...].astype(F32)
        outs[i][...] = total.astype(BF16)


def gradient_own_kernel(decoders, back, low, high, total):
    half = low.shape[1]
    for which, came in ((0, low), (1, high)):
        part = gradient(decoders, back, 0, which, half) + came[...].astype(F32)
        total[:, which * half : (which + 1) * half] = part


def gradient_last_kernel(before, low, high, out):
    half = low.shape[1]
    for which, came in ((0, low), (1, high)):
        part = before[:, which * half : (which + 1) * half] + came[...].astype(F32)
        out[which * half : (which + 1) * half, :] = part.T


def tiled_local(cache, token_ids, enc_weight, enc_bias, dec_weight, dec_bias, incoming, target, returned):
    order, along, shifted = ring_tools()
    size = len(order)
    far = size // 2
    layers = lax.axis_size("section")
    tokens = token_ids.shape[0]
    slots, width = cache.shape[1:]
    mine = enc_weight.shape[1]
    half = mine // 2
    columns = dec_weight.shape[2]
    outs_all = layers * columns
    in_hbm = functools.partial(pltpu.with_memory_space_constraint, memory_space=pltpu.HBM)
    decoders = dec_weight.reshape(outs_all, dec_weight.shape[3])

    block = min(256, half)
    count = mine // block
    low, high = call(
        encode_kernel,
        "encode",
        [((half, tokens), BF16)] * 2,
        [in_hbm(value) for value in (token_ids, cache, enc_weight, enc_bias)],
        [HBM] * 4,
        [
            pltpu.VMEM((1, tokens), jnp.int32),
            pltpu.VMEM((slots, width), BF16),
            pltpu.VMEM((count, block, width), BF16),
            pltpu.VMEM((1, mine), F32),
            pltpu.VMEM((width, tokens), BF16),
            pltpu.SemaphoreType.DMA((count + 3,)),
        ],
        limit=20,
        flops=2 * tokens * width * (mine + slots),
        bytes_accessed=2 * width * (mine + slots),
    )
    piece_flops = 2 * tokens * half * outs_all
    outer = [along(low, 1), along(high, -1)]
    inner = [along(high, 1), along(low, -1)]
    decoders, total = call(
        load_decode_kernel,
        "load_decode",
        [(decoders.shape, BF16), ((outs_all, tokens), F32)],
        (in_hbm(decoders), low, high),
        [HBM] + [VMEM] * 2,
        [pltpu.SemaphoreType.DMA((layers,))],
        flops=2 * piece_flops,
        bytes_accessed=4 * decoders.size,
    )
    for step in range(1, far):
        rise, fall, total = lax.optimization_barrier((*outer, total))
        near = rise, fall
        outer = [along(rise, 1), along(fall, -1)]
        rise, fall, *near = lax.optimization_barrier((*inner, *near))
        if step < far - 1:
            inner = [along(rise, 1), along(fall, -1)]
        for (one, other), which in ((near, 0), ((rise, fall), 1)):
            (total,) = call(
                functools.partial(
                    decode_kernel, pieces=((size - step, which), (step, 1 - which))
                ),
                f"decode_{step}_{which}",
                [((outs_all, tokens), F32)],
                (decoders, total, one, other),
                [VMEM] * 4,
                flops=2 * piece_flops,
            )
    own, *sent = call(
        functools.partial(decode_last_kernel, pieces=((far, 0), (far, 1))),
        "decode_last",
        [((columns, tokens), F32)] + [((columns, tokens), BF16)] * (layers - 1),
        (decoders, total, *outer),
        [VMEM] * 4,
        flops=2 * piece_flops,
    )
    came = [shifted(value, offset) for offset, value in enumerate(sent, 1)]
    error, beyond, *sent = call(
        functools.partial(error_kernel, layers=layers),
        "error",
        [((columns, tokens), BF16), ((columns, tokens), F32)]
        + [((columns, tokens), BF16)] * (layers - 1),
        (own, incoming[0].T, dec_bias, target[0].T, returned[0].T, *came),
        [VMEM] * (layers + 4),
    )
    came = [shifted(value, -offset) for offset, value in enumerate(sent, 1)]
    piece = ((tokens, half), BF16)
    back, *outer = call(
        functools.partial(gradient_first_kernel, layers=layers, pieces=((far, 0), (far, 1))),
        "gradient_far",
        [((tokens, outs_all), BF16), piece, piece],
        (decoders, error, *came),
        [VMEM] * (layers + 1),
        flops=2 * piece_flops,
    )
    inner = []
    for step in range(far - 1, -1, -1):
        outer = [along(outer[0], 1), along(outer[1], -1)]
        if step == 0:
            break
        inner = call(
            functools.partial(gradient_kernel, pieces=((size - step, 0), (step, 1))),
            f"gradient_inner_{step}",
            [piece, piece],
            (decoders, back, *inner),
            [VMEM] * (2 + len(inner)),
            flops=2 * piece_flops,
        )
        inner = [along(inner[0], -1), along(inner[1], 1)]
        outer = call(
            functools.partial(gradient_kernel, pieces=((step, 0), (size - step, 1))),
            f"gradient_outer_{step}",
            [piece, piece],
            (decoders, back, *outer),
            [VMEM] * (2 + len(outer)),
            flops=2 * piece_flops,
        )
    (part,) = call(
        gradient_own_kernel,
        "gradient_own",
        [((tokens, mine), F32)],
        (decoders, back, *inner),
        [VMEM] * 4,
        flops=2 * piece_flops,
    )
    lat_grad = pl.pallas_call(
        gradient_last_kernel,
        out_shape=jax.ShapeDtypeStruct((mine, tokens), F32),
        in_specs=[VMEM] * 3,
        out_specs=VMEM,
        compiler_params=pltpu.CompilerParams(vmem_limit_bytes=4 * 2**20),
        name="gradient_last",
    )(part, *outer)
    return (error.T[None], beyond.T[None], lat_grad[None])


def plain_local(cache, token_ids, enc_weight, enc_bias, dec_weight, dec_bias, incoming, target, returned):
    order, along, shifted = ring_tools()
    size = len(order)
    layers = lax.axis_size("section")
    section = lax.axis_index("section")
    place = jnp.asarray([order.index(i) for i in range(size)], jnp.int32)[lax.axis_index(GROUP)]
    mine = enc_weight.shape[1]
    columns = dec_weight.shape[2]
    tokens = token_ids.shape[0]
    halves = [slice(0, mine // 2), slice(mine // 2, mine)]
    decoders = dec_weight[0].reshape(layers * columns, dec_weight.shape[3])

    def member(distance):
        return jnp.asarray(order, jnp.int32)[(place + distance) % size]

    def part(owner, which):
        start, length = halves[which].start, halves[which].stop - halves[which].start
        return lax.dynamic_slice_in_dim(decoders, owner * mine + start, length, 1)

    def decode(latents, owner, which):
        return lax.dot_general(part(owner, which), latents, NT, preferred_element_type=F32)

    rows = cache[0].at[token_ids].get(mode="promise_in_bounds")
    pre = lax.dot_general(rows, enc_weight[0], NT, preferred_element_type=F32)
    latents = jnp.maximum(pre + enc_bias[0], 0.0).astype(BF16)
    up = [latents[:, cut] for cut in halves]
    down = list(up)
    total = decode(up[0], member(0), 0) + decode(up[1], member(0), 1)
    for step in range(1, (size - 1) // 2 + 1):
        for which in (0, 1):
            up[which] = along(up[which], 1)
            down[which] = along(down[which], -1)
            total = total + decode(up[which], member(-step), which)
            total = total + decode(down[which], member(step), which)
    if size % 2 == 0:
        total = total + decode(along(up[0], 1), member(size // 2), 0)
        total = total + decode(along(down[1], -1), member(size // 2), 1)

    by_offset = total.reshape(layers, columns, tokens)
    within = by_offset[0]
    beyond = jnp.zeros_like(within)
    for offset in range(1, layers):
        came = shifted(by_offset[offset].astype(BF16), offset).astype(F32)
        within = within + jnp.where(section >= offset, came, 0.0)
        beyond = beyond + jnp.where(section < offset, came, 0.0)
    recon = within + incoming[0].T + dec_bias[0][:, None]
    error = (recon - target[0].T.astype(F32)).astype(BF16)
    passed = returned[0].T
    upstream = [error]
    for offset in range(1, layers):
        upstream.append(shifted(jnp.where(section >= offset, error, passed), -offset))
    back = jnp.concatenate(upstream, 0)

    def gradient_of(owner, which):
        return lax.dot_general(part(owner, which), back, TN, preferred_element_type=F32)

    up, down = [None, None], [None, None]
    if size % 2 == 0:
        up[0] = along(gradient_of(member(size // 2), 0).astype(BF16), 1)
        down[1] = along(gradient_of(member(size // 2), 1).astype(BF16), -1)
    for step in range((size - 1) // 2, 0, -1):
        for which in (0, 1):
            rise = gradient_of(member(step), which)
            fall = gradient_of(member(-step), which)
            if up[which] is not None:
                rise = rise + up[which].astype(F32)
            if down[which] is not None:
                fall = fall + down[which].astype(F32)
            up[which] = along(rise.astype(BF16), 1)
            down[which] = along(fall.astype(BF16), -1)
    parts = []
    for which in (0, 1):
        own_part = gradient_of(member(0), which)
        for came in (up[which], down[which]):
            if came is not None:
                own_part = own_part + came.astype(F32)
        parts.append(own_part)
    lat_grad = jnp.concatenate(parts, 0)
    return (error.T[None], beyond.T[None], lat_grad[None])


def local(cache, token_ids, enc_weight, enc_bias, dec_weight, *rest):
    size = lax.axis_size("dp") * lax.axis_size("tensor")
    mine, width = enc_weight.shape[1:]
    whole_tiles = (
        size % 2 == 0
        and size >= 4
        and mine % 256 == 0
        and width % 128 == 0
        and dec_weight.shape[2] % 16 == 0
        and token_ids.shape[0] % 128 == 0
        and cache.shape[1] % 16 == 0
    )
    form = tiled_local if whole_tiles else plain_local
    return form(cache, token_ids, enc_weight, enc_bias, dec_weight, *rest)


def solution(mesh):
    placed = (
        P("section", None, None),
        P(),
        P("section", GROUP, None),
        P("section", GROUP),
        P("section", None, GROUP, None),
        P("section", GROUP),
        P("section", None, GROUP),
        P("section", None, GROUP),
        P("section", None, GROUP),
    )
    return jax.shard_map(
        local,
        mesh=mesh,
        in_specs=placed,
        out_specs=(
            P("section", None, GROUP),
            P("section", None, GROUP),
            P("section", GROUP, None),
        ),
        check_vma=False,
    )
```

```python
import functools

import jax
import jax.numpy as jnp
from jax import lax
from jax.experimental import pallas as pl
from jax.experimental.pallas import tpu as pltpu
from jax.sharding import PartitionSpec as P

GROUP = ("dp", "tensor")
BF16 = jnp.bfloat16
F32 = jnp.float32
VMEM = pl.BlockSpec(memory_space=pltpu.VMEM)
HBM = pl.BlockSpec(memory_space=pltpu.HBM)
NT = (((1,), (1,)), ((), ()))
TN = (((0,), (0,)), ((), ()))


def cycle_order(rows, columns):
    order = []
    for row in range(rows):
        line = [row * columns + column for column in range(columns)]
        order += line if row % 2 == 0 else line[::-1]
    return order


def ring_tools():
    order = cycle_order(lax.axis_size("dp"), lax.axis_size("tensor"))
    size = len(order)
    layers = lax.axis_size("section")

    def along(value, by):
        pairs = [(order[i], order[(i + by) % size]) for i in range(size)]
        return lax.ppermute(value, GROUP, pairs)

    def shifted(value, by):
        return lax.ppermute(value, "section", [(i, (i + by) % layers) for i in range(layers)])

    return order, along, shifted


def call(kernel, name, outs, operands, specs, scratch=(), limit=12, flops=0, bytes_accessed=0):
    return pl.pallas_call(
        kernel,
        out_shape=[pltpu.VMEM(shape, dtype) for shape, dtype in outs],
        in_specs=specs,
        out_specs=[VMEM] * len(outs),
        scratch_shapes=list(scratch),
        compiler_params=pltpu.CompilerParams(vmem_limit_bytes=limit * 2**20),
        cost_estimate=pl.CostEstimate(
            flops=flops, bytes_accessed=bytes_accessed, transcendentals=0
        ),
        name=name,
    )(*operands)


def owner_at(distance):
    rows, line = lax.axis_size("dp"), lax.axis_size("tensor")

    def snake(index):
        row, column = index // line, index % line
        return row * line + jnp.where(row % 2 == 0, column, line - 1 - column)

    place = snake(lax.axis_index("dp") * line + lax.axis_index("tensor"))
    return snake((place + distance) % (rows * line))


def columns_of(decoders, distance, which, count, mine):
    start = owner_at(distance) * mine + which * count
    return decoders[:, pl.ds(pl.multiple_of(start, count), count)]


def upright(row, lanes):
    return jnp.broadcast_to(row, (lanes, row.shape[1])).T


def encode_kernel(ids, cache, weight, bias, latents, ids_, held, blocks, bias_, across, sems):
    count, block = blocks.shape[:2]
    tokens = across.shape[1]
    copies = [
        pltpu.make_async_copy(ids, ids_.at[0], sems.at[count]),
        pltpu.make_async_copy(cache.at[0], held, sems.at[count + 1]),
        pltpu.make_async_copy(bias, bias_, sems.at[count + 2]),
    ]
    for copy in copies:
        copy.start()
    streams = []
    for i in range(count):
        source = weight.at[0, pl.ds(i * block, block)]
        streams.append(pltpu.make_async_copy(source, blocks.at[i], sems.at[i]))
        streams[i].start()
    copies[0].wait()
    slots = lax.broadcasted_iota(jnp.int32, (held.shape[0], tokens), 0)
    picked = (slots == ids_[...]).astype(F32).astype(BF16)
    copies[1].wait()
    rows = lax.dot_general(picked, held[...], TN, preferred_element_type=F32)
    across[...] = rows.astype(BF16).T
    copies[2].wait()
    for i in range(count):
        streams[i].wait()
        pre = jnp.dot(blocks[i], across[...], preferred_element_type=F32)
        pre = pre + upright(bias_[:, i * block : (i + 1) * block], tokens)
        latents[i * block : (i + 1) * block] = jnp.maximum(pre, 0.0).astype(BF16)


def decoded(decoders, pieces):
    total = None
    for distance, which, piece in pieces:
        mine = decoders.shape[1] // (lax.axis_size("dp") * lax.axis_size("tensor"))
        columns = columns_of(decoders, distance, which, piece.shape[0], mine)
        part = jnp.dot(columns, piece[...], preferred_element_type=F32)
        total = part if total is None else total + part
    return total


def load_decode_kernel(source, latents, decoders, total, sems):
    layers = sems.shape[0]
    rows = source.shape[0] // layers
    copies = []
    for i in range(layers):
        part = pl.ds(i * rows, rows)
        copies.append(pltpu.make_async_copy(source.at[part], decoders.at[part], sems.at[i]))
        copies[i].start()
    for i in range(layers):
        part = pl.ds(i * rows, rows)
        copies[i].wait()
        total[part] = decoded(decoders.at[part], [(0, 0, latents)])


def split_kernel(rise, fall, *outs):
    half = rise.shape[0] // 2
    for value, low, high in ((rise, *outs[:2]), (fall, *outs[2:])):
        low[...] = value[:half]
        high[...] = value[half:]


def decode_kernel(decoders, before, one, other, total, *, pieces, layers):
    (d0, w0), (d1, w1) = pieces
    rows = total.shape[0] // layers
    for i in range(layers):
        part = pl.ds(i * rows, rows)
        both = [(d0, w0, one), (d1, w1, other)]
        total[part] = before[part] + decoded(decoders.at[part], both)


def decode_last_kernel(decoders, before, one, other, *outs, pieces):
    (d0, w0), (d1, w1) = pieces
    rows = outs[0].shape[0]
    for i, out in enumerate(outs):
        part = pl.ds(i * rows, rows)
        both = [(d0, w0, one), (d1, w1, other)]
        out[...] = (before[part] + decoded(decoders.at[part], both)).astype(out.dtype)


def error_kernel(own, incoming, bias, target, returned, *refs, layers):
    came, (error, beyond, *sent) = refs[: layers - 1], refs[layers - 1 :]
    section = lax.axis_index("section")
    shift = upright(bias[...], incoming.shape[1])
    within = own[...] + (incoming[...] + shift) - target[...].astype(F32)
    after = jnp.zeros_like(within)
    for offset in range(1, layers):
        part = came[offset - 1][...].astype(F32)
        inside = section >= offset
        within = within + jnp.where(inside, part, 0.0)
        after = after + jnp.where(inside, 0.0, part)
    mine = within.astype(BF16)
    error[...] = mine
    beyond[...] = after
    passed = returned[...]
    for offset in range(1, layers):
        sent[offset - 1][...] = jnp.where(section >= offset, mine, passed)


def gradient(decoders, back, distance, which, half):
    columns = columns_of(decoders, distance, which, half, 2 * half)
    return jnp.dot(back[...], columns, preferred_element_type=F32)


def gradient_first_kernel(decoders, *refs, layers, pieces):
    parts, (back, *outs) = refs[:layers], refs[layers:]
    back[...] = jnp.concatenate([part[...] for part in parts], 0).T
    for (distance, which), out in zip(pieces, outs):
        out[...] = gradient(decoders, back, distance, which, out.shape[1]).astype(BF16)


def gradient_kernel(decoders, back, *outs, pieces):
    for (distance, which), out in zip(pieces, outs):
        part = gradient(decoders, back, distance, which, out.shape[1])
        out[...] = part.astype(out.dtype)


def add_kernel(one, other, came_one, came_other, out_one, out_other):
    out_one[...] = (one[...] + came_one[...].astype(F32)).astype(BF16)
    out_other[...] = (other[...] + came_other[...].astype(F32)).astype(BF16)


def gradient_own_kernel(decoders, back, low, high, total):
    half = low.shape[1]
    for which, came in ((0, low), (1, high)):
        part = gradient(decoders, back, 0, which, half) + came[...].astype(F32)
        total[which * half : (which + 1) * half, :] = part.T


def gradient_last_kernel(before, low, high, out):
    half = low.shape[1]
    for which, came in ((0, low), (1, high)):
        part = slice(which * half, (which + 1) * half)
        out[part, :] = before[part, :] + came[...].T.astype(F32)


def tiled_local(cache, token_ids, enc_weight, enc_bias, dec_weight, dec_bias, incoming, target, returned):
    order, along, shifted = ring_tools()
    size = len(order)
    far = size // 2
    layers = lax.axis_size("section")
    tokens = token_ids.shape[0]
    slots, width = cache.shape[1:]
    mine = enc_weight.shape[1]
    half = mine // 2
    columns = dec_weight.shape[2]
    outs_all = layers * columns
    in_hbm = functools.partial(pltpu.with_memory_space_constraint, memory_space=pltpu.HBM)
    decoders = dec_weight.reshape(outs_all, dec_weight.shape[3])

    block = min(256, half)
    count = mine // block
    (latents,) = call(
        encode_kernel,
        "encode",
        [((mine, tokens), BF16)],
        [in_hbm(value) for value in (token_ids, cache, enc_weight, enc_bias)],
        [HBM] * 4,
        [
            pltpu.VMEM((1, tokens), jnp.int32),
            pltpu.VMEM((slots, width), BF16),
            pltpu.VMEM((count, block, width), BF16),
            pltpu.VMEM((1, mine), F32),
            pltpu.VMEM((width, tokens), BF16),
            pltpu.SemaphoreType.DMA((count + 3,)),
        ],
        limit=24,
        flops=2 * tokens * width * (mine + slots),
        bytes_accessed=2 * width * (mine + slots),
    )
    piece_flops = 2 * tokens * half * outs_all
    rise, fall = along(latents, 1), along(latents, -1)
    held, total = call(
        load_decode_kernel,
        "load_decode",
        [(decoders.shape, BF16), ((outs_all, tokens), F32)],
        (in_hbm(decoders), latents),
        [HBM, VMEM],
        [pltpu.SemaphoreType.DMA((layers,))],
        flops=2 * piece_flops,
        bytes_accessed=4 * decoders.size,
    )

    def decode(name, total, pieces, one, other):
        (total,) = call(
            functools.partial(decode_kernel, pieces=pieces, layers=layers),
            name,
            [((outs_all, tokens), F32)],
            (held, total, one, other),
            [VMEM] * 4,
            flops=2 * piece_flops,
        )
        return total

    rise, fall, total = lax.optimization_barrier((rise, fall, total))
    halves = call(
        split_kernel, "split", [((half, tokens), BF16)] * 4, (rise, fall), [VMEM] * 2
    )
    outer = [along(halves[0], 1), along(halves[3], -1)]
    inner = [along(halves[1], 1), along(halves[2], -1)]
    total = decode("decode_1", total, ((size - 1, 0), (1, 0)), rise, fall)
    for step in range(2, far):
        rise, fall, total = lax.optimization_barrier((*outer, total))
        near = rise, fall
        outer = [along(rise, 1), along(fall, -1)]
        rise, fall, *near = lax.optimization_barrier((*inner, *near))
        if step < far - 1:
            inner = [along(rise, 1), along(fall, -1)]
        total = decode(f"decode_{step}_0", total, ((size - step, 0), (step, 1)), *near)
        pieces = ((size - step, 1), (step, 0))
        total = decode(f"decode_{step}_1", total, pieces, rise, fall)
    own, *sent = call(
        functools.partial(decode_last_kernel, pieces=((far, 0), (far, 1))),
        "decode_last",
        [((columns, tokens), F32)] + [((columns, tokens), BF16)] * (layers - 1),
        (held, total, *outer),
        [VMEM] * 4,
        flops=2 * piece_flops,
    )
    came = [shifted(value, offset) for offset, value in enumerate(sent, 1)]
    error, beyond, *sent = call(
        functools.partial(error_kernel, layers=layers),
        "error",
        [((columns, tokens), BF16), ((columns, tokens), F32)]
        + [((columns, tokens), BF16)] * (layers - 1),
        (own, incoming[0].T, dec_bias, target[0].T, returned[0].T, *came),
        [VMEM] * (layers + 4),
    )
    came = [shifted(value, -offset) for offset, value in enumerate(sent, 1)]
    piece = ((tokens, half), BF16)
    product = ((tokens, half), F32)
    back, *outer = call(
        functools.partial(gradient_first_kernel, layers=layers, pieces=((far, 0), (far, 1))),
        "gradient_far",
        [((tokens, outs_all), BF16), piece, piece],
        (held, error, *came),
        [VMEM] * (layers + 1),
        flops=2 * piece_flops,
    )

    def products(name, kind, pieces, after):
        nonlocal back
        back, *_ = lax.optimization_barrier((back, *after))
        return call(
            functools.partial(gradient_kernel, pieces=pieces),
            name,
            [kind, kind],
            (held, back),
            [VMEM] * 2,
            flops=2 * piece_flops,
        )

    def added(name, parts, came):
        return call(add_kernel, name, [piece, piece], (*parts, *came), [VMEM] * 4)

    last = far - 1
    outer = [along(outer[0], 1), along(outer[1], -1)]
    inner = products("gradient_inner", piece, ((size - last, 0), (last, 1)), ())
    ready = inner
    for step in range(last, 0, -1):
        inner = [along(inner[0], -1), along(inner[1], 1)]
        parts = products(f"outer_{step}", product, ((step, 0), (size - step, 1)), ready)
        ready = added(f"add_outer_{step}", parts, outer)
        outer = [along(ready[0], 1), along(ready[1], -1)]
        if step > 1:
            pieces = ((size - step + 1, 0), (step - 1, 1))
            parts = products(f"inner_{step - 1}", product, pieces, ready)
            inner = ready = added(f"add_inner_{step - 1}", parts, inner)
    (part,) = call(
        gradient_own_kernel,
        "gradient_own",
        [((mine, tokens), F32)],
        (held, back, *inner),
        [VMEM] * 4,
        flops=2 * piece_flops,
    )
    lat_grad = pl.pallas_call(
        gradient_last_kernel,
        out_shape=jax.ShapeDtypeStruct((mine, tokens), F32),
        in_specs=[VMEM] * 3,
        out_specs=VMEM,
        compiler_params=pltpu.CompilerParams(vmem_limit_bytes=12 * 2**20),
        name="gradient_last",
    )(part, *outer)
    return (error.T[None], beyond.T[None], lat_grad[None])


def plain_local(cache, token_ids, enc_weight, enc_bias, dec_weight, dec_bias, incoming, target, returned):
    order, along, shifted = ring_tools()
    size = len(order)
    layers = lax.axis_size("section")
    section = lax.axis_index("section")
    place = jnp.asarray([order.index(i) for i in range(size)], jnp.int32)[lax.axis_index(GROUP)]
    mine = enc_weight.shape[1]
    columns = dec_weight.shape[2]
    tokens = token_ids.shape[0]
    halves = [slice(0, mine // 2), slice(mine // 2, mine)]
    decoders = dec_weight[0].reshape(layers * columns, dec_weight.shape[3])

    def member(distance):
        return jnp.asarray(order, jnp.int32)[(place + distance) % size]

    def part(owner, which):
        start, length = halves[which].start, halves[which].stop - halves[which].start
        return lax.dynamic_slice_in_dim(decoders, owner * mine + start, length, 1)

    def decode(latents, owner, which):
        return lax.dot_general(part(owner, which), latents, NT, preferred_element_type=F32)

    rows = cache[0].at[token_ids].get(mode="promise_in_bounds")
    pre = lax.dot_general(rows, enc_weight[0], NT, preferred_element_type=F32)
    latents = jnp.maximum(pre + enc_bias[0], 0.0).astype(BF16)
    up = [latents[:, cut] for cut in halves]
    down = list(up)
    total = decode(up[0], member(0), 0) + decode(up[1], member(0), 1)
    for step in range(1, (size - 1) // 2 + 1):
        for which in (0, 1):
            up[which] = along(up[which], 1)
            down[which] = along(down[which], -1)
            total = total + decode(up[which], member(-step), which)
            total = total + decode(down[which], member(step), which)
    if size % 2 == 0:
        total = total + decode(along(up[0], 1), member(size // 2), 0)
        total = total + decode(along(down[1], -1), member(size // 2), 1)

    by_offset = total.reshape(layers, columns, tokens)
    within = by_offset[0]
    beyond = jnp.zeros_like(within)
    for offset in range(1, layers):
        came = shifted(by_offset[offset].astype(BF16), offset).astype(F32)
        within = within + jnp.where(section >= offset, came, 0.0)
        beyond = beyond + jnp.where(section < offset, came, 0.0)
    recon = within + incoming[0].T + dec_bias[0][:, None]
    error = (recon - target[0].T.astype(F32)).astype(BF16)
    passed = returned[0].T
    upstream = [error]
    for offset in range(1, layers):
        upstream.append(shifted(jnp.where(section >= offset, error, passed), -offset))
    back = jnp.concatenate(upstream, 0)

    def gradient_of(owner, which):
        return lax.dot_general(part(owner, which), back, TN, preferred_element_type=F32)

    up, down = [None, None], [None, None]
    if size % 2 == 0:
        up[0] = along(gradient_of(member(size // 2), 0).astype(BF16), 1)
        down[1] = along(gradient_of(member(size // 2), 1).astype(BF16), -1)
    for step in range((size - 1) // 2, 0, -1):
        for which in (0, 1):
            rise = gradient_of(member(step), which)
            fall = gradient_of(member(-step), which)
            if up[which] is not None:
                rise = rise + up[which].astype(F32)
            if down[which] is not None:
                fall = fall + down[which].astype(F32)
            up[which] = along(rise.astype(BF16), 1)
            down[which] = along(fall.astype(BF16), -1)
    parts = []
    for which in (0, 1):
        own_part = gradient_of(member(0), which)
        for came in (up[which], down[which]):
            if came is not None:
                own_part = own_part + came.astype(F32)
        parts.append(own_part)
    lat_grad = jnp.concatenate(parts, 0)
    return (error.T[None], beyond.T[None], lat_grad[None])


def local(cache, token_ids, enc_weight, enc_bias, dec_weight, *rest):
    size = lax.axis_size("dp") * lax.axis_size("tensor")
    mine, width = enc_weight.shape[1:]
    whole_tiles = (
        size % 2 == 0
        and size >= 6
        and mine % 256 == 0
        and width % 128 == 0
        and dec_weight.shape[2] % 16 == 0
        and token_ids.shape[0] % 128 == 0
        and cache.shape[1] % 16 == 0
    )
    form = tiled_local if whole_tiles else plain_local
    return form(cache, token_ids, enc_weight, enc_bias, dec_weight, *rest)


def solution(mesh):
    placed = (
        P("section", None, None),
        P(),
        P("section", GROUP, None),
        P("section", GROUP),
        P("section", None, GROUP, None),
        P("section", GROUP),
        P("section", None, GROUP),
        P("section", None, GROUP),
        P("section", None, GROUP),
    )
    return jax.shard_map(
        local,
        mesh=mesh,
        in_specs=placed,
        out_specs=(
            P("section", None, GROUP),
            P("section", None, GROUP),
            P("section", GROUP, None),
        ),
        check_vma=False,
    )
```

```python
import functools

import jax
import jax.numpy as jnp
from jax import lax
from jax.experimental import pallas as pl
from jax.experimental.pallas import tpu as pltpu
from jax.sharding import PartitionSpec as P

GROUP = ("dp", "tensor")
BF16 = jnp.bfloat16
F32 = jnp.float32
VMEM = pl.BlockSpec(memory_space=pltpu.VMEM)
HBM = pl.BlockSpec(memory_space=pltpu.HBM)
NT = (((1,), (1,)), ((), ()))
TN = (((0,), (0,)), ((), ()))


def cycle_order(rows, columns):
    order = []
    for row in range(rows):
        line = [row * columns + column for column in range(columns)]
        order += line if row % 2 == 0 else line[::-1]
    return order


def ring_tools():
    order = cycle_order(lax.axis_size("dp"), lax.axis_size("tensor"))
    size = len(order)
    layers = lax.axis_size("section")

    def along(value, by):
        pairs = [(order[i], order[(i + by) % size]) for i in range(size)]
        return lax.ppermute(value, GROUP, pairs)

    def shifted(value, by):
        return lax.ppermute(value, "section", [(i, (i + by) % layers) for i in range(layers)])

    def swapped(value, bit):
        return lax.ppermute(value, "section", [(i, i ^ bit) for i in range(layers)])

    return order, along, shifted, swapped


def call(kernel, name, outs, operands, specs, scratch=(), limit=12, flops=0, bytes_accessed=0):
    return pl.pallas_call(
        kernel,
        out_shape=[pltpu.VMEM(shape, dtype) for shape, dtype in outs],
        in_specs=specs,
        out_specs=[VMEM] * len(outs),
        scratch_shapes=list(scratch),
        compiler_params=pltpu.CompilerParams(vmem_limit_bytes=limit * 2**20),
        cost_estimate=pl.CostEstimate(
            flops=flops, bytes_accessed=bytes_accessed, transcendentals=0
        ),
        name=name,
    )(*operands)


def owner_at(distance):
    rows, line = lax.axis_size("dp"), lax.axis_size("tensor")

    def snake(index):
        row, column = index // line, index % line
        return row * line + jnp.where(row % 2 == 0, column, line - 1 - column)

    place = snake(lax.axis_index("dp") * line + lax.axis_index("tensor"))
    return snake((place + distance) % (rows * line))


def columns_of(decoders, distance, which, count, mine):
    start = owner_at(distance) * mine + which * count
    return decoders[:, pl.ds(pl.multiple_of(start, count), count)]


def upright(row, lanes):
    return jnp.broadcast_to(row, (lanes, row.shape[1])).T


def encode_kernel(ids, cache, weight, bias, latents, ids_, held, blocks, bias_, across, sems):
    count, block = blocks.shape[:2]
    tokens = across.shape[1]
    copies = [
        pltpu.make_async_copy(ids, ids_.at[0], sems.at[count]),
        pltpu.make_async_copy(cache.at[0], held, sems.at[count + 1]),
        pltpu.make_async_copy(bias, bias_, sems.at[count + 2]),
    ]
    for copy in copies:
        copy.start()
    streams = []
    for i in range(count):
        source = weight.at[0, pl.ds(i * block, block)]
        streams.append(pltpu.make_async_copy(source, blocks.at[i], sems.at[i]))
        streams[i].start()
    copies[0].wait()
    slots = lax.broadcasted_iota(jnp.int32, (held.shape[0], tokens), 0)
    picked = (slots == ids_[...]).astype(F32).astype(BF16)
    copies[1].wait()
    rows = lax.dot_general(picked, held[...], TN, preferred_element_type=F32)
    across[...] = rows.astype(BF16).T
    copies[2].wait()
    for i in range(count):
        streams[i].wait()
        pre = jnp.dot(blocks[i], across[...], preferred_element_type=F32)
        pre = pre + upright(bias_[:, i * block : (i + 1) * block], tokens)
        latents[i * block : (i + 1) * block] = jnp.maximum(pre, 0.0).astype(BF16)


def decoded(decoders, pieces):
    total = None
    for distance, which, piece in pieces:
        mine = decoders.shape[1] // (lax.axis_size("dp") * lax.axis_size("tensor"))
        columns = columns_of(decoders, distance, which, piece.shape[0], mine)
        part = jnp.dot(columns, piece[...], preferred_element_type=F32)
        total = part if total is None else total + part
    return total


def load_decode_kernel(source, latents, decoders, total, sems):
    layers = sems.shape[0]
    rows = source.shape[0] // layers
    copies = []
    for i in range(layers):
        part = pl.ds(i * rows, rows)
        copies.append(pltpu.make_async_copy(source.at[part], decoders.at[part], sems.at[i]))
        copies[i].start()
    for i in range(layers):
        part = pl.ds(i * rows, rows)
        copies[i].wait()
        total[part] = decoded(decoders.at[part], [(0, 0, latents)])


def split_kernel(rise, fall, *outs):
    half = rise.shape[0] // 2
    for value, low, high in ((rise, *outs[:2]), (fall, *outs[2:])):
        low[...] = value[:half]
        high[...] = value[half:]


def decode_kernel(decoders, before, one, other, total, *, pieces, layers):
    (d0, w0), (d1, w1) = pieces
    rows = total.shape[0] // layers
    for i in range(layers):
        part = pl.ds(i * rows, rows)
        both = [(d0, w0, one), (d1, w1, other)]
        total[part] = before[part] + decoded(decoders.at[part], both)


def decode_last_kernel(decoders, before, one, other, total, sent, *, pieces, layers):
    decode_kernel(decoders, before, one, other, total, pieces=pieces, layers=layers)
    sent[...] = total[...].astype(BF16)


def ahead_kernel(incoming, bias, target, returned, base, sent):
    shift = upright(bias[...], incoming.shape[1])
    base[...] = incoming[...] + shift - target[...].astype(F32)
    sent[...] = jnp.where(lax.axis_index("section") < 2, returned[...], base[...].astype(BF16))


def ahead_pair_kernel(base, returned, came, sent):
    rows = base.shape[0]
    even = lax.axis_index("section") % 2 == 0
    sent[:rows] = jnp.where(even, came[...], base[...].astype(BF16))
    sent[rows:] = jnp.where(even, returned[...], came[...])


def chip_sum_kernel(total, mate, sums, sent, after):
    section = lax.axis_index("section")
    rows = after.shape[0]
    even = section % 2 == 0
    for reach in range(5):
        part = None
        for offset, mine in ((reach, even), (reach - 1, jnp.logical_not(even))):
            if 0 <= offset < 4:
                cut = pl.ds(offset * rows, rows)
                value = jnp.where(mine, total[cut], mate[cut].astype(F32))
                part = value if part is None else part + value
        sums[pl.ds(reach * rows, rows)] = part
    for i in range(2):
        lower, upper = sums[pl.ds((2 + i) * rows, rows)], sums[pl.ds(i * rows, rows)]
        sent[pl.ds(i * rows, rows)] = jnp.where(section < 2, lower, upper).astype(BF16)
    after[...] = jnp.where(even, sums[pl.ds(2 * rows, rows)], sums[pl.ds(3 * rows, rows)]).astype(BF16)


def error_kernel(decoders, base, sums, across, first, pair, back, error, *outs, pieces):
    section = lax.axis_index("section")
    rows = base.shape[0]
    low_chip = section < 2
    recon = [sums[pl.ds(layer * rows, rows)] for layer in range(2)]
    for i in range(2):
        whole = jnp.where(low_chip, sums[pl.ds((2 + i) * rows, rows)], recon[i])
        recon.append(whole + across[pl.ds(i * rows, rows)].astype(F32))
    starts = [base[...], pair[:rows].astype(F32), first[...].astype(F32), pair[rows:].astype(F32)]
    upstream = []
    for offset, start in enumerate(starts):
        part = jnp.zeros_like(start)
        for layer in range(offset, 4):
            part = jnp.where(section + offset == layer, recon[layer], part)
        upstream.append((start + part).astype(BF16))
    error[...] = upstream[0]
    back[...] = jnp.concatenate(upstream, 0).T
    for (distance, which), out in zip(pieces, outs):
        out[...] = gradient(decoders, back, distance, which, out.shape[1]).astype(BF16)


def outgoing_kernel(sums, came, beyond):
    section = lax.axis_index("section")
    rows = beyond.shape[0]
    own = jnp.where(section % 2 == 0, sums[pl.ds(4 * rows, rows)], 0.0)
    beyond[...] = own + jnp.where(section < 2, came[...].astype(F32), 0.0)


def gradient(decoders, back, distance, which, half):
    columns = columns_of(decoders, distance, which, half, 2 * half)
    return jnp.dot(back[...], columns, preferred_element_type=F32)


def gradient_kernel(decoders, back, *outs, pieces):
    for (distance, which), out in zip(pieces, outs):
        part = gradient(decoders, back, distance, which, out.shape[1])
        out[...] = part.astype(out.dtype)


def add_kernel(one, other, came_one, came_other, out_one, out_other):
    out_one[...] = (one[...] + came_one[...].astype(F32)).astype(BF16)
    out_other[...] = (other[...] + came_other[...].astype(F32)).astype(BF16)


def gradient_own_kernel(decoders, back, low, high, total):
    half = low.shape[1]
    for which, came in ((0, low), (1, high)):
        part = gradient(decoders, back, 0, which, half) + came[...].astype(F32)
        total[which * half : (which + 1) * half, :] = part.T


def gradient_last_kernel(before, low, high, out):
    half = low.shape[1]
    for which, came in ((0, low), (1, high)):
        part = slice(which * half, (which + 1) * half)
        out[part, :] = before[part, :] + came[...].T.astype(F32)


def tiled_local(cache, token_ids, enc_weight, enc_bias, dec_weight, dec_bias, incoming, target, returned):
    order, along, _, swapped = ring_tools()
    size = len(order)
    far = size // 2
    layers = lax.axis_size("section")
    tokens = token_ids.shape[0]
    slots, width = cache.shape[1:]
    mine = enc_weight.shape[1]
    half = mine // 2
    columns = dec_weight.shape[2]
    outs_all = layers * columns
    in_hbm = functools.partial(pltpu.with_memory_space_constraint, memory_space=pltpu.HBM)
    decoders = dec_weight.reshape(outs_all, dec_weight.shape[3])

    block = min(256, half)
    count = mine // block
    (latents,) = call(
        encode_kernel,
        "encode",
        [((mine, tokens), BF16)],
        [in_hbm(value) for value in (token_ids, cache, enc_weight, enc_bias)],
        [HBM] * 4,
        [
            pltpu.VMEM((1, tokens), jnp.int32),
            pltpu.VMEM((slots, width), BF16),
            pltpu.VMEM((count, block, width), BF16),
            pltpu.VMEM((1, mine), F32),
            pltpu.VMEM((width, tokens), BF16),
            pltpu.SemaphoreType.DMA((count + 3,)),
        ],
        limit=24,
        flops=2 * tokens * width * (mine + slots),
        bytes_accessed=2 * width * (mine + slots),
    )
    piece_flops = 2 * tokens * half * outs_all
    rise, fall = along(latents, 1), along(latents, -1)
    held, total = call(
        load_decode_kernel,
        "load_decode",
        [(decoders.shape, BF16), ((outs_all, tokens), F32)],
        (in_hbm(decoders), latents),
        [HBM, VMEM],
        [pltpu.SemaphoreType.DMA((layers,))],
        flops=2 * piece_flops,
        bytes_accessed=4 * decoders.size,
    )

    def decode(name, total, pieces, one, other):
        (total,) = call(
            functools.partial(decode_kernel, pieces=pieces, layers=layers),
            name,
            [((outs_all, tokens), F32)],
            (held, total, one, other),
            [VMEM] * 4,
            flops=2 * piece_flops,
        )
        return total

    rise, fall, total = lax.optimization_barrier((rise, fall, total))
    halves = call(
        split_kernel, "split", [((half, tokens), BF16)] * 4, (rise, fall), [VMEM] * 2
    )
    outer = [along(halves[0], 1), along(halves[3], -1)]
    inner = [along(halves[1], 1), along(halves[2], -1)]
    total = decode("decode_1", total, ((size - 1, 0), (1, 0)), rise, fall)
    base, sent = call(
        ahead_kernel,
        "ahead",
        [((columns, tokens), F32), ((columns, tokens), BF16)],
        (incoming[0].T, dec_bias, target[0].T, returned[0].T),
        [VMEM] * 4,
    )
    first = swapped(sent, 2)
    for step in range(2, far):
        rise, fall, total = lax.optimization_barrier((*outer, total))
        near = rise, fall
        outer = [along(rise, 1), along(fall, -1)]
        if step == 2:
            first, *inner = lax.optimization_barrier((first, *inner))
        rise, fall, *near = lax.optimization_barrier((*inner, *near))
        if step < far - 1:
            inner = [along(rise, 1), along(fall, -1)]
        total = decode(f"decode_{step}_0", total, ((size - step, 0), (step, 1)), *near)
        pieces = ((size - step, 1), (step, 0))
        total = decode(f"decode_{step}_1", total, pieces, rise, fall)
    (sent,) = call(
        ahead_pair_kernel,
        "ahead_pair",
        [((2 * columns, tokens), BF16)],
        (base, returned[0].T, first),
        [VMEM] * 3,
    )
    pair = swapped(sent, 1)
    *outer, pair = lax.optimization_barrier((*outer, pair))
    total, sent = call(
        functools.partial(decode_last_kernel, pieces=((far, 0), (far, 1)), layers=layers),
        "decode_last",
        [((outs_all, tokens), F32), ((outs_all, tokens), BF16)],
        (held, total, *outer),
        [VMEM] * 4,
        flops=2 * piece_flops,
    )
    sums, sent, after = call(
        chip_sum_kernel,
        "chip_sum",
        [
            (((layers + 1) * columns, tokens), F32),
            ((2 * columns, tokens), BF16),
            ((columns, tokens), BF16),
        ],
        (total, swapped(sent, 1)),
        [VMEM] * 2,
    )
    across = swapped(sent, 2)
    piece = ((tokens, half), BF16)
    product = ((tokens, half), F32)
    back, error, *outer = call(
        functools.partial(error_kernel, pieces=((far, 0), (far, 1))),
        "error",
        [((tokens, outs_all), BF16), ((columns, tokens), BF16), piece, piece],
        (held, base, sums, across, first, pair),
        [VMEM] * 6,
        flops=2 * piece_flops,
    )

    def products(name, kind, pieces, after):
        nonlocal back
        back, *_ = lax.optimization_barrier((back, *after))
        return call(
            functools.partial(gradient_kernel, pieces=pieces),
            name,
            [kind, kind],
            (held, back),
            [VMEM] * 2,
            flops=2 * piece_flops,
        )

    def added(name, parts, came):
        return call(add_kernel, name, [piece, piece], (*parts, *came), [VMEM] * 4)

    last = far - 1
    outer = [along(outer[0], 1), along(outer[1], -1)]
    inner = products("gradient_inner", piece, ((size - last, 0), (last, 1)), ())
    ready = inner
    after, *_ = lax.optimization_barrier((after, *inner))
    came = swapped(after, 2)
    for step in range(last, 0, -1):
        inner = [along(inner[0], -1), along(inner[1], 1)]
        if step == last - 1:
            back, came = lax.optimization_barrier((back, came))
        parts = products(f"outer_{step}", product, ((step, 0), (size - step, 1)), ready)
        ready = added(f"add_outer_{step}", parts, outer)
        outer = [along(ready[0], 1), along(ready[1], -1)]
        if step > 1:
            pieces = ((size - step + 1, 0), (step - 1, 1))
            parts = products(f"inner_{step - 1}", product, pieces, ready)
            inner = ready = added(f"add_inner_{step - 1}", parts, inner)
    (beyond,) = call(
        outgoing_kernel,
        "outgoing",
        [((columns, tokens), F32)],
        (sums, came),
        [VMEM] * 2,
    )
    (part,) = call(
        gradient_own_kernel,
        "gradient_own",
        [((mine, tokens), F32)],
        (held, back, *inner),
        [VMEM] * 4,
        flops=2 * piece_flops,
    )
    lat_grad = pl.pallas_call(
        gradient_last_kernel,
        out_shape=jax.ShapeDtypeStruct((mine, tokens), F32),
        in_specs=[VMEM] * 3,
        out_specs=VMEM,
        compiler_params=pltpu.CompilerParams(vmem_limit_bytes=12 * 2**20),
        name="gradient_last",
    )(part, *outer)
    return (error.T[None], beyond.T[None], lat_grad[None])


def plain_local(cache, token_ids, enc_weight, enc_bias, dec_weight, dec_bias, incoming, target, returned):
    order, along, shifted, _ = ring_tools()
    size = len(order)
    layers = lax.axis_size("section")
    section = lax.axis_index("section")
    place = jnp.asarray([order.index(i) for i in range(size)], jnp.int32)[lax.axis_index(GROUP)]
    mine = enc_weight.shape[1]
    columns = dec_weight.shape[2]
    tokens = token_ids.shape[0]
    halves = [slice(0, mine // 2), slice(mine // 2, mine)]
    decoders = dec_weight[0].reshape(layers * columns, dec_weight.shape[3])

    def member(distance):
        return jnp.asarray(order, jnp.int32)[(place + distance) % size]

    def part(owner, which):
        start, length = halves[which].start, halves[which].stop - halves[which].start
        return lax.dynamic_slice_in_dim(decoders, owner * mine + start, length, 1)

    def decode(latents, owner, which):
        return lax.dot_general(part(owner, which), latents, NT, preferred_element_type=F32)

    rows = cache[0].at[token_ids].get(mode="promise_in_bounds")
    pre = lax.dot_general(rows, enc_weight[0], NT, preferred_element_type=F32)
    latents = jnp.maximum(pre + enc_bias[0], 0.0).astype(BF16)
    up = [latents[:, cut] for cut in halves]
    down = list(up)
    total = decode(up[0], member(0), 0) + decode(up[1], member(0), 1)
    for step in range(1, (size - 1) // 2 + 1):
        for which in (0, 1):
            up[which] = along(up[which], 1)
            down[which] = along(down[which], -1)
            total = total + decode(up[which], member(-step), which)
            total = total + decode(down[which], member(step), which)
    if size % 2 == 0:
        total = total + decode(along(up[0], 1), member(size // 2), 0)
        total = total + decode(along(down[1], -1), member(size // 2), 1)

    by_offset = total.reshape(layers, columns, tokens)
    within = by_offset[0]
    beyond = jnp.zeros_like(within)
    for offset in range(1, layers):
        came = shifted(by_offset[offset].astype(BF16), offset).astype(F32)
        within = within + jnp.where(section >= offset, came, 0.0)
        beyond = beyond + jnp.where(section < offset, came, 0.0)
    recon = within + incoming[0].T + dec_bias[0][:, None]
    error = (recon - target[0].T.astype(F32)).astype(BF16)
    passed = returned[0].T
    upstream = [error]
    for offset in range(1, layers):
        upstream.append(shifted(jnp.where(section >= offset, error, passed), -offset))
    back = jnp.concatenate(upstream, 0)

    def gradient_of(owner, which):
        return lax.dot_general(part(owner, which), back, TN, preferred_element_type=F32)

    up, down = [None, None], [None, None]
    if size % 2 == 0:
        up[0] = along(gradient_of(member(size // 2), 0).astype(BF16), 1)
        down[1] = along(gradient_of(member(size // 2), 1).astype(BF16), -1)
    for step in range((size - 1) // 2, 0, -1):
        for which in (0, 1):
            rise = gradient_of(member(step), which)
            fall = gradient_of(member(-step), which)
            if up[which] is not None:
                rise = rise + up[which].astype(F32)
            if down[which] is not None:
                fall = fall + down[which].astype(F32)
            up[which] = along(rise.astype(BF16), 1)
            down[which] = along(fall.astype(BF16), -1)
    parts = []
    for which in (0, 1):
        own_part = gradient_of(member(0), which)
        for came in (up[which], down[which]):
            if came is not None:
                own_part = own_part + came.astype(F32)
        parts.append(own_part)
    lat_grad = jnp.concatenate(parts, 0)
    return (error.T[None], beyond.T[None], lat_grad[None])


def local(cache, token_ids, enc_weight, enc_bias, dec_weight, *rest):
    size = lax.axis_size("dp") * lax.axis_size("tensor")
    mine, width = enc_weight.shape[1:]
    whole_tiles = (
        size % 2 == 0
        and size >= 6
        and lax.axis_size("section") == 4
        and mine % 256 == 0
        and width % 128 == 0
        and dec_weight.shape[2] % 16 == 0
        and token_ids.shape[0] % 128 == 0
        and cache.shape[1] % 16 == 0
    )
    form = tiled_local if whole_tiles else plain_local
    return form(cache, token_ids, enc_weight, enc_bias, dec_weight, *rest)


def solution(mesh):
    placed = (
        P("section", None, None),
        P(),
        P("section", GROUP, None),
        P("section", GROUP),
        P("section", None, GROUP, None),
        P("section", GROUP),
        P("section", None, GROUP),
        P("section", None, GROUP),
        P("section", None, GROUP),
    )
    return jax.shard_map(
        local,
        mesh=mesh,
        in_specs=placed,
        out_specs=(
            P("section", None, GROUP),
            P("section", None, GROUP),
            P("section", GROUP, None),
        ),
        check_vma=False,
    )
```

```python
import functools

import jax
import jax.numpy as jnp
from jax import lax
from jax.experimental import pallas as pl
from jax.experimental.pallas import tpu as pltpu
from jax.sharding import PartitionSpec as P

GROUP = ("dp", "tensor")
BF16 = jnp.bfloat16
F32 = jnp.float32
VMEM = pl.BlockSpec(memory_space=pltpu.VMEM)
HBM = pl.BlockSpec(memory_space=pltpu.HBM)
NT = (((1,), (1,)), ((), ()))
TN = (((0,), (0,)), ((), ()))


def cycle_order(rows, columns):
    order = []
    for row in range(rows):
        line = [row * columns + column for column in range(columns)]
        order += line if row % 2 == 0 else line[::-1]
    return order


def ring_tools():
    order = cycle_order(lax.axis_size("dp"), lax.axis_size("tensor"))
    size = len(order)
    layers = lax.axis_size("section")

    def along(value, by):
        pairs = [(order[i], order[(i + by) % size]) for i in range(size)]
        return lax.ppermute(value, GROUP, pairs)

    def shifted(value, by):
        return lax.ppermute(value, "section", [(i, (i + by) % layers) for i in range(layers)])

    def swapped(value, bit):
        return lax.ppermute(value, "section", [(i, i ^ bit) for i in range(layers)])

    return order, along, shifted, swapped


def call(kernel, name, outs, operands, specs, scratch=(), limit=12, flops=0, bytes_accessed=0):
    return pl.pallas_call(
        kernel,
        out_shape=[pltpu.VMEM(shape, dtype) for shape, dtype in outs],
        in_specs=specs,
        out_specs=[VMEM] * len(outs),
        scratch_shapes=list(scratch),
        compiler_params=pltpu.CompilerParams(vmem_limit_bytes=limit * 2**20),
        cost_estimate=pl.CostEstimate(
            flops=flops, bytes_accessed=bytes_accessed, transcendentals=0
        ),
        name=name,
    )(*operands)


def owner_at(distance):
    rows, line = lax.axis_size("dp"), lax.axis_size("tensor")

    def snake(index):
        row, column = index // line, index % line
        return row * line + jnp.where(row % 2 == 0, column, line - 1 - column)

    place = snake(lax.axis_index("dp") * line + lax.axis_index("tensor"))
    return snake((place + distance) % (rows * line))


def columns_of(decoders, distance, which, count, mine):
    start = owner_at(distance) * mine + which * count
    return decoders[:, pl.ds(pl.multiple_of(start, count), count)]


def upright(row, lanes):
    return jnp.broadcast_to(row, (lanes, row.shape[1])).T


def encode_kernel(ids, cache, weight, bias, latents, ids_, held, blocks, bias_, across, sems):
    count, block = blocks.shape[:2]
    tokens = across.shape[1]
    copies = [
        pltpu.make_async_copy(ids, ids_.at[0], sems.at[count]),
        pltpu.make_async_copy(cache.at[0], held, sems.at[count + 1]),
        pltpu.make_async_copy(bias, bias_, sems.at[count + 2]),
    ]
    for copy in copies:
        copy.start()
    streams = []
    for i in range(count):
        source = weight.at[0, pl.ds(i * block, block)]
        streams.append(pltpu.make_async_copy(source, blocks.at[i], sems.at[i]))
        streams[i].start()
    copies[0].wait()
    slots = lax.broadcasted_iota(jnp.int32, (held.shape[0], tokens), 0)
    picked = (slots == ids_[...]).astype(F32).astype(BF16)
    copies[1].wait()
    rows = lax.dot_general(picked, held[...], TN, preferred_element_type=F32)
    across[...] = rows.astype(BF16).T
    copies[2].wait()
    for i in range(count):
        streams[i].wait()
        pre = jnp.dot(blocks[i], across[...], preferred_element_type=F32)
        pre = pre + upright(bias_[:, i * block : (i + 1) * block], tokens)
        latents[i * block : (i + 1) * block] = jnp.maximum(pre, 0.0).astype(BF16)


def decoded(decoders, pieces):
    total = None
    for distance, which, piece in pieces:
        mine = decoders.shape[1] // (lax.axis_size("dp") * lax.axis_size("tensor"))
        columns = columns_of(decoders, distance, which, piece.shape[0], mine)
        part = jnp.dot(columns, piece[...], preferred_element_type=F32)
        total = part if total is None else total + part
    return total


def load_decode_kernel(source, latents, decoders, total, sems):
    layers = sems.shape[0]
    rows = source.shape[0] // layers
    copies = []
    for i in range(layers):
        part = pl.ds(i * rows, rows)
        copies.append(pltpu.make_async_copy(source.at[part], decoders.at[part], sems.at[i]))
        copies[i].start()
    for i in range(layers):
        part = pl.ds(i * rows, rows)
        copies[i].wait()
        total[part] = decoded(decoders.at[part], [(0, 0, latents)])


def split_kernel(rise, fall, *outs):
    half = rise.shape[0] // 2
    for value, low, high in ((rise, *outs[:2]), (fall, *outs[2:])):
        low[...] = value[:half]
        high[...] = value[half:]


def decode_kernel(decoders, before, one, other, total, *, pieces, layers):
    (d0, w0), (d1, w1) = pieces
    rows = total.shape[0] // layers
    for i in range(layers):
        part = pl.ds(i * rows, rows)
        both = [(d0, w0, one), (d1, w1, other)]
        total[part] = before[part] + decoded(decoders.at[part], both)


def decode_last_kernel(decoders, before, one, other, total, sent, *, pieces, layers):
    decode_kernel(decoders, before, one, other, total, pieces=pieces, layers=layers)
    sent[...] = total[...].astype(BF16)


def ahead_kernel(incoming, bias, target, returned, base, sent):
    shift = upright(bias[...], incoming.shape[1])
    base[...] = incoming[...] + shift - target[...].astype(F32)
    sent[...] = jnp.where(lax.axis_index("section") < 2, returned[...], base[...].astype(BF16))


def ahead_pair_kernel(base, returned, came, sent):
    rows = base.shape[0]
    even = lax.axis_index("section") % 2 == 0
    sent[:rows] = jnp.where(even, came[...], base[...].astype(BF16))
    sent[rows:] = jnp.where(even, returned[...], came[...])


def chip_sum_kernel(total, mate, sums, sent, after):
    section = lax.axis_index("section")
    rows = after.shape[0]
    even = section % 2 == 0
    for reach in range(5):
        part = None
        for offset, mine in ((reach, even), (reach - 1, jnp.logical_not(even))):
            if 0 <= offset < 4:
                cut = pl.ds(offset * rows, rows)
                value = jnp.where(mine, total[cut], mate[cut].astype(F32))
                part = value if part is None else part + value
        sums[pl.ds(reach * rows, rows)] = part
    for i in range(2):
        lower, upper = sums[pl.ds((2 + i) * rows, rows)], sums[pl.ds(i * rows, rows)]
        sent[pl.ds(i * rows, rows)] = jnp.where(section < 2, lower, upper).astype(BF16)
    after[...] = jnp.where(even, sums[pl.ds(2 * rows, rows)], sums[pl.ds(3 * rows, rows)]).astype(BF16)


def error_kernel(decoders, base, sums, across, first, pair, back, error, *outs, pieces):
    section = lax.axis_index("section")
    rows = base.shape[0]
    low_chip = section < 2
    recon = [sums[pl.ds(layer * rows, rows)] for layer in range(2)]
    for i in range(2):
        whole = jnp.where(low_chip, sums[pl.ds((2 + i) * rows, rows)], recon[i])
        recon.append(whole + across[pl.ds(i * rows, rows)].astype(F32))
    starts = [base[...], pair[:rows].astype(F32), first[...].astype(F32), pair[rows:].astype(F32)]
    upstream = []
    for offset, start in enumerate(starts):
        part = jnp.zeros_like(start)
        for layer in range(offset, 4):
            part = jnp.where(section + offset == layer, recon[layer], part)
        upstream.append((start + part).astype(BF16))
    error[...] = upstream[0]
    back[...] = jnp.concatenate(upstream, 0).T
    for (distance, which), out in zip(pieces, outs):
        out[...] = gradient(decoders, back, distance, which, out.shape[1]).astype(BF16)


def outgoing_kernel(sums, came, beyond):
    section = lax.axis_index("section")
    rows = beyond.shape[0]
    own = jnp.where(section % 2 == 0, sums[pl.ds(4 * rows, rows)], 0.0)
    beyond[...] = own + jnp.where(section < 2, came[...].astype(F32), 0.0)


def gradient(decoders, back, distance, which, half):
    columns = columns_of(decoders, distance, which, half, 2 * half)
    return jnp.dot(back[...], columns, preferred_element_type=F32)


def gradient_kernel(decoders, back, *outs, pieces):
    for (distance, which), out in zip(pieces, outs):
        part = gradient(decoders, back, distance, which, out.shape[1])
        out[...] = part.astype(out.dtype)


def add_kernel(one, other, came_one, came_other, out_one, out_other):
    out_one[...] = (one[...] + came_one[...].astype(F32)).astype(BF16)
    out_other[...] = (other[...] + came_other[...].astype(F32)).astype(BF16)


def gradient_own_kernel(decoders, back, low, high, total):
    half = low.shape[1]
    for which, came in ((0, low), (1, high)):
        part = gradient(decoders, back, 0, which, half) + came[...].astype(F32)
        total[which * half : (which + 1) * half, :] = part.T


def gradient_last_kernel(before, low, high, out):
    half = low.shape[1]
    for which, came in ((0, low), (1, high)):
        part = slice(which * half, (which + 1) * half)
        out[part, :] = before[part, :] + came[...].T.astype(F32)


def tiled_local(cache, token_ids, enc_weight, enc_bias, dec_weight, dec_bias, incoming, target, returned):
    order, along, _, swapped = ring_tools()
    size = len(order)
    far = size // 2
    layers = lax.axis_size("section")
    tokens = token_ids.shape[0]
    slots, width = cache.shape[1:]
    mine = enc_weight.shape[1]
    half = mine // 2
    columns = dec_weight.shape[2]
    outs_all = layers * columns
    in_hbm = functools.partial(pltpu.with_memory_space_constraint, memory_space=pltpu.HBM)
    decoders = dec_weight.reshape(outs_all, dec_weight.shape[3])

    block = min(256, half)
    count = mine // block
    (latents,) = call(
        encode_kernel,
        "encode",
        [((mine, tokens), BF16)],
        [in_hbm(value) for value in (token_ids, cache, enc_weight, enc_bias)],
        [HBM] * 4,
        [
            pltpu.VMEM((1, tokens), jnp.int32),
            pltpu.VMEM((slots, width), BF16),
            pltpu.VMEM((count, block, width), BF16),
            pltpu.VMEM((1, mine), F32),
            pltpu.VMEM((width, tokens), BF16),
            pltpu.SemaphoreType.DMA((count + 3,)),
        ],
        limit=24,
        flops=2 * tokens * width * (mine + slots),
        bytes_accessed=2 * width * (mine + slots),
    )
    piece_flops = 2 * tokens * half * outs_all
    rise, fall = along(latents, 1), along(latents, -1)
    held, total = call(
        load_decode_kernel,
        "load_decode",
        [(decoders.shape, BF16), ((outs_all, tokens), F32)],
        (in_hbm(decoders), latents),
        [HBM, VMEM],
        [pltpu.SemaphoreType.DMA((layers,))],
        flops=2 * piece_flops,
        bytes_accessed=4 * decoders.size,
    )

    def decode(name, total, pieces, one, other):
        (total,) = call(
            functools.partial(decode_kernel, pieces=pieces, layers=layers),
            name,
            [((outs_all, tokens), F32)],
            (held, total, one, other),
            [VMEM] * 4,
            flops=2 * piece_flops,
        )
        return total

    rise, fall, total = lax.optimization_barrier((rise, fall, total))
    halves = call(
        split_kernel, "split", [((half, tokens), BF16)] * 4, (rise, fall), [VMEM] * 2
    )
    outer = [along(halves[0], 1), along(halves[3], -1)]
    total = decode("decode_1", total, ((size - 1, 0), (1, 0)), rise, fall)
    one, other, total = lax.optimization_barrier((halves[1], halves[2], total))
    inner = [along(one, 1), along(other, -1)]
    base, sent = call(
        ahead_kernel,
        "ahead",
        [((columns, tokens), F32), ((columns, tokens), BF16)],
        (incoming[0].T, dec_bias, target[0].T, returned[0].T),
        [VMEM] * 4,
    )
    for step in range(2, far):
        tied = (sent, total) if step == 2 else ()
        rise, fall, *tied = lax.optimization_barrier((*outer, *tied))
        near = rise, fall
        outer = [along(rise, 1), along(fall, -1)]
        if step == 2:
            sent, total = tied
            first = swapped(sent, 2)
            first, *inner = lax.optimization_barrier((first, *inner))
        rise, fall, *near = lax.optimization_barrier((*inner, *near))
        if step < far - 1:
            inner = [along(rise, 1), along(fall, -1)]
        total = decode(f"decode_{step}_0", total, ((size - step, 0), (step, 1)), *near)
        pieces = ((size - step, 1), (step, 0))
        total = decode(f"decode_{step}_1", total, pieces, rise, fall)
    (sent,) = call(
        ahead_pair_kernel,
        "ahead_pair",
        [((2 * columns, tokens), BF16)],
        (base, returned[0].T, first),
        [VMEM] * 3,
    )
    pair = swapped(sent, 1)
    *outer, pair = lax.optimization_barrier((*outer, pair))
    total, sent = call(
        functools.partial(decode_last_kernel, pieces=((far, 0), (far, 1)), layers=layers),
        "decode_last",
        [((outs_all, tokens), F32), ((outs_all, tokens), BF16)],
        (held, total, *outer),
        [VMEM] * 4,
        flops=2 * piece_flops,
    )
    sums, sent, after = call(
        chip_sum_kernel,
        "chip_sum",
        [
            (((layers + 1) * columns, tokens), F32),
            ((2 * columns, tokens), BF16),
            ((columns, tokens), BF16),
        ],
        (total, swapped(sent, 1)),
        [VMEM] * 2,
    )
    across = swapped(sent, 2)
    piece = ((tokens, half), BF16)
    product = ((tokens, half), F32)
    back, error, *outer = call(
        functools.partial(error_kernel, pieces=((far, 0), (far, 1))),
        "error",
        [((tokens, outs_all), BF16), ((columns, tokens), BF16), piece, piece],
        (held, base, sums, across, first, pair),
        [VMEM] * 6,
        flops=2 * piece_flops,
    )

    def products(name, kind, pieces, after):
        nonlocal back
        back, *_ = lax.optimization_barrier((back, *after))
        return call(
            functools.partial(gradient_kernel, pieces=pieces),
            name,
            [kind, kind],
            (held, back),
            [VMEM] * 2,
            flops=2 * piece_flops,
        )

    def added(name, parts, came):
        return call(add_kernel, name, [piece, piece], (*parts, *came), [VMEM] * 4)

    last = far - 1
    outer = [along(outer[0], 1), along(outer[1], -1)]
    inner = products("gradient_inner", piece, ((size - last, 0), (last, 1)), ())
    ready = inner
    after, *_ = lax.optimization_barrier((after, *inner))
    came = swapped(after, 2)
    for step in range(last, 0, -1):
        inner = [along(inner[0], -1), along(inner[1], 1)]
        if step == last - 1:
            back, came = lax.optimization_barrier((back, came))
        parts = products(f"outer_{step}", product, ((step, 0), (size - step, 1)), ready)
        ready = added(f"add_outer_{step}", parts, outer)
        outer = [along(ready[0], 1), along(ready[1], -1)]
        if step > 1:
            pieces = ((size - step + 1, 0), (step - 1, 1))
            parts = products(f"inner_{step - 1}", product, pieces, ready)
            inner = ready = added(f"add_inner_{step - 1}", parts, inner)
    (beyond,) = call(
        outgoing_kernel,
        "outgoing",
        [((columns, tokens), F32)],
        (sums, came),
        [VMEM] * 2,
    )
    (part,) = call(
        gradient_own_kernel,
        "gradient_own",
        [((mine, tokens), F32)],
        (held, back, *inner),
        [VMEM] * 4,
        flops=2 * piece_flops,
    )
    lat_grad = pl.pallas_call(
        gradient_last_kernel,
        out_shape=jax.ShapeDtypeStruct((mine, tokens), F32),
        in_specs=[VMEM] * 3,
        out_specs=VMEM,
        compiler_params=pltpu.CompilerParams(vmem_limit_bytes=12 * 2**20),
        name="gradient_last",
    )(part, *outer)
    return (error.T[None], beyond.T[None], lat_grad[None])


def plain_local(cache, token_ids, enc_weight, enc_bias, dec_weight, dec_bias, incoming, target, returned):
    order, along, shifted, _ = ring_tools()
    size = len(order)
    layers = lax.axis_size("section")
    section = lax.axis_index("section")
    place = jnp.asarray([order.index(i) for i in range(size)], jnp.int32)[lax.axis_index(GROUP)]
    mine = enc_weight.shape[1]
    columns = dec_weight.shape[2]
    tokens = token_ids.shape[0]
    halves = [slice(0, mine // 2), slice(mine // 2, mine)]
    decoders = dec_weight[0].reshape(layers * columns, dec_weight.shape[3])

    def member(distance):
        return jnp.asarray(order, jnp.int32)[(place + distance) % size]

    def part(owner, which):
        start, length = halves[which].start, halves[which].stop - halves[which].start
        return lax.dynamic_slice_in_dim(decoders, owner * mine + start, length, 1)

    def decode(latents, owner, which):
        return lax.dot_general(part(owner, which), latents, NT, preferred_element_type=F32)

    rows = cache[0].at[token_ids].get(mode="promise_in_bounds")
    pre = lax.dot_general(rows, enc_weight[0], NT, preferred_element_type=F32)
    latents = jnp.maximum(pre + enc_bias[0], 0.0).astype(BF16)
    up = [latents[:, cut] for cut in halves]
    down = list(up)
    total = decode(up[0], member(0), 0) + decode(up[1], member(0), 1)
    for step in range(1, (size - 1) // 2 + 1):
        for which in (0, 1):
            up[which] = along(up[which], 1)
            down[which] = along(down[which], -1)
            total = total + decode(up[which], member(-step), which)
            total = total + decode(down[which], member(step), which)
    if size % 2 == 0:
        total = total + decode(along(up[0], 1), member(size // 2), 0)
        total = total + decode(along(down[1], -1), member(size // 2), 1)

    by_offset = total.reshape(layers, columns, tokens)
    within = by_offset[0]
    beyond = jnp.zeros_like(within)
    for offset in range(1, layers):
        came = shifted(by_offset[offset].astype(BF16), offset).astype(F32)
        within = within + jnp.where(section >= offset, came, 0.0)
        beyond = beyond + jnp.where(section < offset, came, 0.0)
    recon = within + incoming[0].T + dec_bias[0][:, None]
    error = (recon - target[0].T.astype(F32)).astype(BF16)
    passed = returned[0].T
    upstream = [error]
    for offset in range(1, layers):
        upstream.append(shifted(jnp.where(section >= offset, error, passed), -offset))
    back = jnp.concatenate(upstream, 0)

    def gradient_of(owner, which):
        return lax.dot_general(part(owner, which), back, TN, preferred_element_type=F32)

    up, down = [None, None], [None, None]
    if size % 2 == 0:
        up[0] = along(gradient_of(member(size // 2), 0).astype(BF16), 1)
        down[1] = along(gradient_of(member(size // 2), 1).astype(BF16), -1)
    for step in range((size - 1) // 2, 0, -1):
        for which in (0, 1):
            rise = gradient_of(member(step), which)
            fall = gradient_of(member(-step), which)
            if up[which] is not None:
                rise = rise + up[which].astype(F32)
            if down[which] is not None:
                fall = fall + down[which].astype(F32)
            up[which] = along(rise.astype(BF16), 1)
            down[which] = along(fall.astype(BF16), -1)
    parts = []
    for which in (0, 1):
        own_part = gradient_of(member(0), which)
        for came in (up[which], down[which]):
            if came is not None:
                own_part = own_part + came.astype(F32)
        parts.append(own_part)
    lat_grad = jnp.concatenate(parts, 0)
    return (error.T[None], beyond.T[None], lat_grad[None])


def local(cache, token_ids, enc_weight, enc_bias, dec_weight, *rest):
    size = lax.axis_size("dp") * lax.axis_size("tensor")
    mine, width = enc_weight.shape[1:]
    whole_tiles = (
        size % 2 == 0
        and size >= 6
        and lax.axis_size("section") == 4
        and mine % 256 == 0
        and width % 128 == 0
        and dec_weight.shape[2] % 16 == 0
        and token_ids.shape[0] % 128 == 0
        and cache.shape[1] % 16 == 0
    )
    form = tiled_local if whole_tiles else plain_local
    return form(cache, token_ids, enc_weight, enc_bias, dec_weight, *rest)


def solution(mesh):
    placed = (
        P("section", None, None),
        P(),
        P("section", GROUP, None),
        P("section", GROUP),
        P("section", None, GROUP, None),
        P("section", GROUP),
        P("section", None, GROUP),
        P("section", None, GROUP),
        P("section", None, GROUP),
    )
    return jax.shard_map(
        local,
        mesh=mesh,
        in_specs=placed,
        out_specs=(
            P("section", None, GROUP),
            P("section", None, GROUP),
            P("section", GROUP, None),
        ),
        check_vma=False,
    )
```

```python
import functools

import jax
import jax.numpy as jnp
from jax import lax
from jax.experimental import pallas as pl
from jax.experimental.pallas import tpu as pltpu
from jax.sharding import PartitionSpec as P

GROUP = ("dp", "tensor")
BF16 = jnp.bfloat16
F32 = jnp.float32
VMEM = pl.BlockSpec(memory_space=pltpu.VMEM)
HBM = pl.BlockSpec(memory_space=pltpu.HBM)
NT = (((1,), (1,)), ((), ()))
TN = (((0,), (0,)), ((), ()))


def cycle_order(rows, columns):
    order = []
    for row in range(rows):
        line = [row * columns + column for column in range(columns)]
        order += line if row % 2 == 0 else line[::-1]
    return order


def ring_tools():
    order = cycle_order(lax.axis_size("dp"), lax.axis_size("tensor"))
    size = len(order)
    layers = lax.axis_size("section")

    def along(value, by):
        pairs = [(order[i], order[(i + by) % size]) for i in range(size)]
        return lax.ppermute(value, GROUP, pairs)

    def shifted(value, by):
        return lax.ppermute(value, "section", [(i, (i + by) % layers) for i in range(layers)])

    def swapped(value, bit):
        return lax.ppermute(value, "section", [(i, i ^ bit) for i in range(layers)])

    return order, along, shifted, swapped


def call(kernel, name, outs, operands, specs, scratch=(), limit=12, flops=0, bytes_accessed=0):
    return pl.pallas_call(
        kernel,
        out_shape=[pltpu.VMEM(shape, dtype) for shape, dtype in outs],
        in_specs=specs,
        out_specs=[VMEM] * len(outs),
        scratch_shapes=list(scratch),
        compiler_params=pltpu.CompilerParams(vmem_limit_bytes=limit * 2**20),
        cost_estimate=pl.CostEstimate(
            flops=flops, bytes_accessed=bytes_accessed, transcendentals=0
        ),
        name=name,
    )(*operands)


def owner_at(distance):
    rows, line = lax.axis_size("dp"), lax.axis_size("tensor")

    def snake(index):
        row, column = index // line, index % line
        return row * line + jnp.where(row % 2 == 0, column, line - 1 - column)

    place = snake(lax.axis_index("dp") * line + lax.axis_index("tensor"))
    return snake((place + distance) % (rows * line))


def columns_of(decoders, distance, which, count, mine):
    start = owner_at(distance) * mine + which * count
    return decoders[:, pl.ds(pl.multiple_of(start, count), count)]


def upright(row, lanes):
    return jnp.broadcast_to(row, (lanes, row.shape[1])).T


def encode_kernel(ids, cache, weight, bias, latents, ids_, held, blocks, bias_, across, sems):
    count, block = blocks.shape[:2]
    tokens = across.shape[1]
    copies = [
        pltpu.make_async_copy(ids, ids_.at[0], sems.at[count]),
        pltpu.make_async_copy(cache.at[0], held, sems.at[count + 1]),
        pltpu.make_async_copy(bias, bias_, sems.at[count + 2]),
    ]
    for copy in copies:
        copy.start()
    streams = []
    for i in range(count):
        source = weight.at[0, pl.ds(i * block, block)]
        streams.append(pltpu.make_async_copy(source, blocks.at[i], sems.at[i]))
        streams[i].start()
    copies[0].wait()
    slots = lax.broadcasted_iota(jnp.int32, (held.shape[0], tokens), 0)
    picked = (slots == ids_[...]).astype(F32).astype(BF16)
    copies[1].wait()
    rows = lax.dot_general(picked, held[...], TN, preferred_element_type=F32)
    across[...] = rows.astype(BF16).T
    copies[2].wait()
    for i in range(count):
        streams[i].wait()
        pre = jnp.dot(blocks[i], across[...], preferred_element_type=F32)
        pre = pre + upright(bias_[:, i * block : (i + 1) * block], tokens)
        latents[i * block : (i + 1) * block] = jnp.maximum(pre, 0.0).astype(BF16)


def decoded(decoders, pieces):
    total = None
    for distance, which, piece in pieces:
        mine = decoders.shape[1] // (lax.axis_size("dp") * lax.axis_size("tensor"))
        columns = columns_of(decoders, distance, which, piece.shape[0], mine)
        part = jnp.dot(columns, piece[...], preferred_element_type=F32)
        total = part if total is None else total + part
    return total


def load_decode_kernel(source, latents, decoders, total, sems):
    layers = sems.shape[0]
    rows = source.shape[0] // layers
    copies = []
    for i in range(layers):
        part = pl.ds(i * rows, rows)
        copies.append(pltpu.make_async_copy(source.at[part], decoders.at[part], sems.at[i]))
        copies[i].start()
    for i in range(layers):
        part = pl.ds(i * rows, rows)
        copies[i].wait()
        total[part] = decoded(decoders.at[part], [(0, 0, latents)])


def split_kernel(rise, fall, *outs):
    half = rise.shape[0] // 2
    for value, low, high in ((rise, *outs[:2]), (fall, *outs[2:])):
        low[...] = value[:half]
        high[...] = value[half:]


def decode_kernel(decoders, before, one, other, total, *, pieces, layers):
    (d0, w0), (d1, w1) = pieces
    rows = total.shape[0] // layers
    for i in range(layers):
        part = pl.ds(i * rows, rows)
        both = [(d0, w0, one), (d1, w1, other)]
        total[part] = before[part] + decoded(decoders.at[part], both)


def decode_last_kernel(decoders, before, one, other, total, sent, *, pieces, layers):
    decode_kernel(decoders, before, one, other, total, pieces=pieces, layers=layers)
    sent[...] = total[...].astype(BF16)


def ahead_kernel(incoming, bias, target, returned, base, sent):
    shift = upright(bias[...], incoming.shape[1])
    base[...] = incoming[...] + shift - target[...].astype(F32)
    sent[...] = jnp.where(lax.axis_index("section") < 2, returned[...], base[...].astype(BF16))


def ahead_pair_kernel(base, returned, came, sent):
    rows = base.shape[0]
    even = lax.axis_index("section") % 2 == 0
    sent[:rows] = jnp.where(even, came[...], base[...].astype(BF16))
    sent[rows:] = jnp.where(even, returned[...], came[...])


def chip_sum_kernel(total, mate, sums, sent, after):
    section = lax.axis_index("section")
    rows = after.shape[0]
    even = section % 2 == 0
    for reach in range(5):
        part = None
        for offset, mine in ((reach, even), (reach - 1, jnp.logical_not(even))):
            if 0 <= offset < 4:
                cut = pl.ds(offset * rows, rows)
                value = jnp.where(mine, total[cut], mate[cut].astype(F32))
                part = value if part is None else part + value
        sums[pl.ds(reach * rows, rows)] = part
    for i in range(2):
        lower, upper = sums[pl.ds((2 + i) * rows, rows)], sums[pl.ds(i * rows, rows)]
        sent[pl.ds(i * rows, rows)] = jnp.where(section < 2, lower, upper).astype(BF16)
    after[...] = jnp.where(even, sums[pl.ds(2 * rows, rows)], sums[pl.ds(3 * rows, rows)]).astype(BF16)


def error_kernel(decoders, base, sums, across, first, pair, back, error, *outs, pieces):
    section = lax.axis_index("section")
    rows = base.shape[0]
    low_chip = section < 2
    recon = [sums[pl.ds(layer * rows, rows)] for layer in range(2)]
    for i in range(2):
        whole = jnp.where(low_chip, sums[pl.ds((2 + i) * rows, rows)], recon[i])
        recon.append(whole + across[pl.ds(i * rows, rows)].astype(F32))
    starts = [base[...], pair[:rows].astype(F32), first[...].astype(F32), pair[rows:].astype(F32)]
    upstream = []
    for offset, start in enumerate(starts):
        part = jnp.zeros_like(start)
        for layer in range(offset, 4):
            part = jnp.where(section + offset == layer, recon[layer], part)
        upstream.append((start + part).astype(BF16))
    error[...] = upstream[0]
    back[...] = jnp.concatenate(upstream, 0).T
    for (distance, which), out in zip(pieces, outs):
        out[...] = gradient(decoders, back, distance, which, out.shape[1]).astype(BF16)


def outgoing_kernel(sums, came, beyond):
    section = lax.axis_index("section")
    rows = beyond.shape[0]
    own = jnp.where(section % 2 == 0, sums[pl.ds(4 * rows, rows)], 0.0)
    beyond[...] = own + jnp.where(section < 2, came[...].astype(F32), 0.0)


def gradient(decoders, back, distance, which, half):
    columns = columns_of(decoders, distance, which, half, 2 * half)
    return jnp.dot(back[...], columns, preferred_element_type=F32)


def gradient_kernel(decoders, back, *outs, pieces):
    for (distance, which), out in zip(pieces, outs):
        part = gradient(decoders, back, distance, which, out.shape[1])
        out[...] = part.astype(out.dtype)


def add_kernel(one, other, came_one, came_other, out_one, out_other):
    out_one[...] = (one[...] + came_one[...].astype(F32)).astype(BF16)
    out_other[...] = (other[...] + came_other[...].astype(F32)).astype(BF16)


def gradient_own_kernel(decoders, back, low, high, total):
    half = low.shape[1]
    for which, came in ((0, low), (1, high)):
        part = gradient(decoders, back, 0, which, half) + came[...].astype(F32)
        total[which * half : (which + 1) * half, :] = part.T


def gradient_last_kernel(before, low, high, out):
    half = low.shape[1]
    for which, came in ((0, low), (1, high)):
        part = slice(which * half, (which + 1) * half)
        out[part, :] = before[part, :] + came[...].T.astype(F32)


def tiled_local(cache, token_ids, enc_weight, enc_bias, dec_weight, dec_bias, incoming, target, returned):
    order, along, _, swapped = ring_tools()
    size = len(order)
    far = size // 2
    layers = lax.axis_size("section")
    tokens = token_ids.shape[0]
    slots, width = cache.shape[1:]
    mine = enc_weight.shape[1]
    half = mine // 2
    columns = dec_weight.shape[2]
    outs_all = layers * columns
    in_hbm = functools.partial(pltpu.with_memory_space_constraint, memory_space=pltpu.HBM)
    decoders = dec_weight.reshape(outs_all, dec_weight.shape[3])

    block = min(256, half)
    count = mine // block
    (latents,) = call(
        encode_kernel,
        "encode",
        [((mine, tokens), BF16)],
        [in_hbm(value) for value in (token_ids, cache, enc_weight, enc_bias)],
        [HBM] * 4,
        [
            pltpu.VMEM((1, tokens), jnp.int32),
            pltpu.VMEM((slots, width), BF16),
            pltpu.VMEM((count, block, width), BF16),
            pltpu.VMEM((1, mine), F32),
            pltpu.VMEM((width, tokens), BF16),
            pltpu.SemaphoreType.DMA((count + 3,)),
        ],
        limit=24,
        flops=2 * tokens * width * (mine + slots),
        bytes_accessed=2 * width * (mine + slots),
    )
    piece_flops = 2 * tokens * half * outs_all
    rise, fall = along(latents, 1), along(latents, -1)
    held, total = call(
        load_decode_kernel,
        "load_decode",
        [(decoders.shape, BF16), ((outs_all, tokens), F32)],
        (in_hbm(decoders), latents),
        [HBM, VMEM],
        [pltpu.SemaphoreType.DMA((layers,))],
        flops=2 * piece_flops,
        bytes_accessed=4 * decoders.size,
    )

    def decode(name, total, pieces, one, other):
        (total,) = call(
            functools.partial(decode_kernel, pieces=pieces, layers=layers),
            name,
            [((outs_all, tokens), F32)],
            (held, total, one, other),
            [VMEM] * 4,
            flops=2 * piece_flops,
        )
        return total

    rise, fall, total = lax.optimization_barrier((rise, fall, total))
    halves = call(
        split_kernel, "split", [((half, tokens), BF16)] * 4, (rise, fall), [VMEM] * 2
    )
    outer = [along(halves[0], 1), along(halves[3], -1)]
    total = decode("decode_1", total, ((size - 1, 0), (1, 0)), rise, fall)
    one, other, total = lax.optimization_barrier((halves[1], halves[2], total))
    inner = [along(one, 1), along(other, -1)]
    base, sent = call(
        ahead_kernel,
        "ahead",
        [((columns, tokens), F32), ((columns, tokens), BF16)],
        (incoming[0].T, dec_bias, target[0].T, returned[0].T),
        [VMEM] * 4,
    )
    for step in range(2, far):
        tied = (sent, total) if step == 2 else ()
        rise, fall, *tied = lax.optimization_barrier((*outer, *tied))
        near = rise, fall
        outer = [along(rise, 1), along(fall, -1)]
        if step == 2:
            sent, total = tied
            first = swapped(sent, 2)
            first, *inner = lax.optimization_barrier((first, *inner))
        rise, fall, *near = lax.optimization_barrier((*inner, *near))
        if step < far - 1:
            inner = [along(rise, 1), along(fall, -1)]
        total = decode(f"decode_{step}_0", total, ((size - step, 0), (step, 1)), *near)
        pieces = ((size - step, 1), (step, 0))
        total = decode(f"decode_{step}_1", total, pieces, rise, fall)
    (sent,) = call(
        ahead_pair_kernel,
        "ahead_pair",
        [((2 * columns, tokens), BF16)],
        (base, returned[0].T, first),
        [VMEM] * 3,
    )
    pair = swapped(sent, 1)
    *outer, pair = lax.optimization_barrier((*outer, pair))
    total, sent = call(
        functools.partial(decode_last_kernel, pieces=((far, 0), (far, 1)), layers=layers),
        "decode_last",
        [((outs_all, tokens), F32), ((outs_all, tokens), BF16)],
        (held, total, *outer),
        [VMEM] * 4,
        flops=2 * piece_flops,
    )
    sums, sent, after = call(
        chip_sum_kernel,
        "chip_sum",
        [
            (((layers + 1) * columns, tokens), F32),
            ((2 * columns, tokens), BF16),
            ((columns, tokens), BF16),
        ],
        (total, swapped(sent, 1)),
        [VMEM] * 2,
    )
    across = swapped(sent, 2)
    piece = ((tokens, half), BF16)
    product = ((tokens, half), F32)
    back, error, *outer = call(
        functools.partial(error_kernel, pieces=((far, 0), (far, 1))),
        "error",
        [((tokens, outs_all), BF16), ((columns, tokens), BF16), piece, piece],
        (held, base, sums, across, first, pair),
        [VMEM] * 6,
        flops=2 * piece_flops,
    )

    def products(name, kind, pieces, after):
        nonlocal back
        back, *_ = lax.optimization_barrier((back, *after))
        return call(
            functools.partial(gradient_kernel, pieces=pieces),
            name,
            [kind] * len(pieces),
            (held, back),
            [VMEM] * 2,
            flops=len(pieces) * piece_flops,
        )

    def added(name, parts, came):
        return call(add_kernel, name, [piece, piece], (*parts, *came), [VMEM] * 4)

    last = far - 1
    outer = [along(outer[0], 1), along(outer[1], -1)]
    inner = products("gradient_inner", piece, ((size - last, 0), (last, 1)), ())
    ready = inner
    after, *_ = lax.optimization_barrier((after, *inner))
    came = swapped(after, 2)
    for step in range(last, 0, -1):
        inner = [along(inner[0], -1), along(inner[1], 1)]
        if step == last - 1:
            back, came = lax.optimization_barrier((back, came))
        pieces = ((step, 0), (size - step, 1))
        if step > 1:
            pieces += ((size - step + 1, 0), (step - 1, 1))
        parts = products(f"products_{step}", product, pieces, ready)
        ready = added(f"add_outer_{step}", parts[:2], outer)
        outer = [along(ready[0], 1), along(ready[1], -1)]
        if step > 1:
            inner = ready = added(f"add_inner_{step - 1}", parts[2:], inner)
    (beyond,) = call(
        outgoing_kernel,
        "outgoing",
        [((columns, tokens), F32)],
        (sums, came),
        [VMEM] * 2,
    )
    (part,) = call(
        gradient_own_kernel,
        "gradient_own",
        [((mine, tokens), F32)],
        (held, back, *inner),
        [VMEM] * 4,
        flops=2 * piece_flops,
    )
    lat_grad = pl.pallas_call(
        gradient_last_kernel,
        out_shape=jax.ShapeDtypeStruct((mine, tokens), F32),
        in_specs=[VMEM] * 3,
        out_specs=VMEM,
        compiler_params=pltpu.CompilerParams(vmem_limit_bytes=12 * 2**20),
        name="gradient_last",
    )(part, *outer)
    return (error.T[None], beyond.T[None], lat_grad[None])


def plain_local(cache, token_ids, enc_weight, enc_bias, dec_weight, dec_bias, incoming, target, returned):
    order, along, shifted, _ = ring_tools()
    size = len(order)
    layers = lax.axis_size("section")
    section = lax.axis_index("section")
    place = jnp.asarray([order.index(i) for i in range(size)], jnp.int32)[lax.axis_index(GROUP)]
    mine = enc_weight.shape[1]
    columns = dec_weight.shape[2]
    tokens = token_ids.shape[0]
    halves = [slice(0, mine // 2), slice(mine // 2, mine)]
    decoders = dec_weight[0].reshape(layers * columns, dec_weight.shape[3])

    def member(distance):
        return jnp.asarray(order, jnp.int32)[(place + distance) % size]

    def part(owner, which):
        start, length = halves[which].start, halves[which].stop - halves[which].start
        return lax.dynamic_slice_in_dim(decoders, owner * mine + start, length, 1)

    def decode(latents, owner, which):
        return lax.dot_general(part(owner, which), latents, NT, preferred_element_type=F32)

    rows = cache[0].at[token_ids].get(mode="promise_in_bounds")
    pre = lax.dot_general(rows, enc_weight[0], NT, preferred_element_type=F32)
    latents = jnp.maximum(pre + enc_bias[0], 0.0).astype(BF16)
    up = [latents[:, cut] for cut in halves]
    down = list(up)
    total = decode(up[0], member(0), 0) + decode(up[1], member(0), 1)
    for step in range(1, (size - 1) // 2 + 1):
        for which in (0, 1):
            up[which] = along(up[which], 1)
            down[which] = along(down[which], -1)
            total = total + decode(up[which], member(-step), which)
            total = total + decode(down[which], member(step), which)
    if size % 2 == 0:
        total = total + decode(along(up[0], 1), member(size // 2), 0)
        total = total + decode(along(down[1], -1), member(size // 2), 1)

    by_offset = total.reshape(layers, columns, tokens)
    within = by_offset[0]
    beyond = jnp.zeros_like(within)
    for offset in range(1, layers):
        came = shifted(by_offset[offset].astype(BF16), offset).astype(F32)
        within = within + jnp.where(section >= offset, came, 0.0)
        beyond = beyond + jnp.where(section < offset, came, 0.0)
    recon = within + incoming[0].T + dec_bias[0][:, None]
    error = (recon - target[0].T.astype(F32)).astype(BF16)
    passed = returned[0].T
    upstream = [error]
    for offset in range(1, layers):
        upstream.append(shifted(jnp.where(section >= offset, error, passed), -offset))
    back = jnp.concatenate(upstream, 0)

    def gradient_of(owner, which):
        return lax.dot_general(part(owner, which), back, TN, preferred_element_type=F32)

    up, down = [None, None], [None, None]
    if size % 2 == 0:
        up[0] = along(gradient_of(member(size // 2), 0).astype(BF16), 1)
        down[1] = along(gradient_of(member(size // 2), 1).astype(BF16), -1)
    for step in range((size - 1) // 2, 0, -1):
        for which in (0, 1):
            rise = gradient_of(member(step), which)
            fall = gradient_of(member(-step), which)
            if up[which] is not None:
                rise = rise + up[which].astype(F32)
            if down[which] is not None:
                fall = fall + down[which].astype(F32)
            up[which] = along(rise.astype(BF16), 1)
            down[which] = along(fall.astype(BF16), -1)
    parts = []
    for which in (0, 1):
        own_part = gradient_of(member(0), which)
        for came in (up[which], down[which]):
            if came is not None:
                own_part = own_part + came.astype(F32)
        parts.append(own_part)
    lat_grad = jnp.concatenate(parts, 0)
    return (error.T[None], beyond.T[None], lat_grad[None])


def local(cache, token_ids, enc_weight, enc_bias, dec_weight, *rest):
    size = lax.axis_size("dp") * lax.axis_size("tensor")
    mine, width = enc_weight.shape[1:]
    whole_tiles = (
        size % 2 == 0
        and size >= 6
        and lax.axis_size("section") == 4
        and mine % 256 == 0
        and width % 128 == 0
        and dec_weight.shape[2] % 16 == 0
        and token_ids.shape[0] % 128 == 0
        and cache.shape[1] % 16 == 0
    )
    form = tiled_local if whole_tiles else plain_local
    return form(cache, token_ids, enc_weight, enc_bias, dec_weight, *rest)


def solution(mesh):
    placed = (
        P("section", None, None),
        P(),
        P("section", GROUP, None),
        P("section", GROUP),
        P("section", None, GROUP, None),
        P("section", GROUP),
        P("section", None, GROUP),
        P("section", None, GROUP),
        P("section", None, GROUP),
    )
    return jax.shard_map(
        local,
        mesh=mesh,
        in_specs=placed,
        out_specs=(
            P("section", None, GROUP),
            P("section", None, GROUP),
            P("section", GROUP, None),
        ),
        check_vma=False,
    )
```
